256 devices in a mesh: region: 16 (over z, core), patch: 16 (over y, x).
Axes of the slice: x: 4, y: 4, z: 8, core: 2. Of those that a mesh axis runs over, the one named last changes fastest.
Arguments:
- coarse: float32 [70, 128, 128, 128], P(None, 'region', 'patch'), may hold values from -6 to 6
- fine_patches: bfloat16 [512, 70, 4096], P(('region', 'patch')), may hold values from -6 to 6
- new_owner: int32 [512, 1], P(('region', 'patch')), may hold values from 0 to 15, as said below
- corners: int32 [512, 3], P(('region', 'patch')), may hold values from 0 to 120
- level_tags: int32 [512], P(('region', 'patch')), may hold values from 1 to 2
- diffusivity: float32 [70], replicated, may hold values from 0.005 to 0.05
- velocity: float32 [3], replicated, may hold values from 0.05 to 0.2
- growth_weight: float32 [40, 30], replicated, may hold values from -1 to 1
- yield_weight: float32 [30, 40], replicated, may hold values from -1 to 1
Outputs:
- coarse_next: float32 [70, 128, 128, 128], P(None, 'region', 'patch')
- fine_next: bfloat16 [1024, 70, 4096], P(('region', 'patch'))
The draws below stay inside these ranges and needn't reach their ends.
Inputs may be any that keep to these rules, and one draw needn't show every extreme that they name: `new_owner`: in each region two owners receive exactly 4 patches, two receive none and the others 2; each device sends both of its patches to one owner.
All inputs are finite; a program needn't handle non-finite values.
Results may differ from the reference program's by a relative error of at most 0.001.
Values may be sent and summed in bfloat16 or wider, within the bound.
A program may use at most 192 MiB of HBM per device.

```python
import math
import jax
import jax.numpy as jnp
from jax import lax

F_SOOT = 40
F_SPEC = 30
FIELDS = 70
B = 16
P_DEV = 2
CZ = 8
CX = 8
NY = 128
RECV = 4
PATCHES = 512
SLOTS = 1024
NZ = 128
NX = 128
N_REGION = 16
N_PATCH = 16


def draw_corners(key, part):
    key = jax.random.fold_in(key, 11)
    first, second, third = jax.random.split(key, 3)
    along_z = jax.random.randint(first, (PATCHES, 1), 0, CZ - B // 2 + 1)
    along_x = jax.random.randint(second, (PATCHES, 1), 0, CX - B // 2 + 1)
    along_y = jax.random.randint(third, (PATCHES, 1), 0, NY - B // 2 + 1)
    return jnp.concatenate([along_z, along_x, along_y], axis=1).astype(jnp.int32)


def owners_of_region(order_key, column_key):
    order = jax.random.permutation(order_key, N_PATCH)
    place = jnp.arange(N_PATCH)
    share = jnp.where(place < 2, 2 * P_DEV, jnp.where(place < 4, 0, P_DEV)).astype(jnp.int32)
    load = jnp.zeros((N_PATCH,), jnp.int32).at[order].set(share)
    ends = jnp.cumsum(load)
    position = jnp.arange(N_PATCH * P_DEV)
    owner = jnp.sum((ends[None, :] <= position[:, None]).astype(jnp.int32), axis=1)
    pair_index = position // 2
    columns = jax.random.permutation(column_key, N_PATCH)
    sender = columns[pair_index % N_PATCH]
    within = 2 * (pair_index // N_PATCH) + position % 2
    return jnp.zeros((N_PATCH, P_DEV), jnp.int32).at[sender, within].set(owner.astype(jnp.int32))


def draw_new_owner(key, part):
    key = jax.random.fold_in(key, 5)
    first, second = jax.random.split(key, 2)
    region_keys = jax.random.split(first, N_REGION)
    column_keys = jax.random.split(second, N_REGION)
    grid = jax.vmap(owners_of_region)(region_keys, column_keys)
    return grid.reshape(PATCHES, 1).astype(jnp.int32)


def plant(values, rng, low, top_value):
    longest = values.shape.index(max(values.shape))
    spots = []
    for shift in (0, 1):
        where = [jax.random.randint(jax.random.fold_in(rng, axis), (), 0, length) for axis, length in enumerate(values.shape)]
        where[longest] = (where[longest] + shift) % values.shape[longest]
        spots.append(tuple(where))
    return values.at[spots[0]].set(low).at[spots[1]].set(top_value)


def steps_of(rng, extent, shards, low, largest):
    factor_of, own = 1.0, jax.random.fold_in(rng, 6)
    for dim, blocks in shards:
        heights = jnp.exp(jax.random.uniform(jax.random.fold_in(own, dim), (blocks,), jnp.float32, low / len(shards), largest / len(shards)))
        factor_of = factor_of * jnp.repeat(heights, extent[dim] // blocks).reshape([-1 if axis == dim else 1 for axis in range(len(extent))])
    return factor_of


def scatter_about(own_key, extent, deviation, reach, cuts=(), kind=jnp.bfloat16):
    values = deviation * jax.random.normal(own_key, extent, jnp.float32)
    if cuts:
        values = values * steps_of(own_key, extent, cuts, -0.22, 0.18)
    return jnp.clip(values, -reach, reach).astype(kind)


def setup_inputs(seed: int = 0) -> dict:
    arg_keys = jax.random.split(jax.random.key(seed), 10)
    return {
        "coarse": scatter_about(arg_keys[0], (FIELDS, NZ, NX, NY), 1.0, 6.0, ((1, 16), (2, 16)), jnp.float32),
        "fine_patches": scatter_about(arg_keys[1], (PATCHES, FIELDS, B ** 3), 1.0, 6.0, ((0, 256),)),
        "new_owner": draw_new_owner(jax.random.fold_in(arg_keys[9], 71), 0),
        "corners": draw_corners(jax.random.fold_in(arg_keys[9], 71), 0),
        "level_tags": plant(jax.random.randint(arg_keys[4], (PATCHES,), 1, 3), jax.random.fold_in(arg_keys[4], 1), 1, 2).astype(jnp.int32),
        "diffusivity": jnp.clip(jnp.exp(jax.random.uniform(arg_keys[5], (FIELDS,), jnp.float32, math.log(0.005), math.log(0.05))), 0.005, 0.05),
        "velocity": jnp.clip(jnp.exp(jax.random.uniform(arg_keys[6], (3,), jnp.float32, math.log(0.05), math.log(0.2))), 0.05, 0.2),
        "growth_weight": scatter_about(arg_keys[7], (F_SOOT, F_SPEC), F_SPEC ** -0.5, 1.0, (), jnp.float32),
        "yield_weight": scatter_about(arg_keys[8], (F_SPEC, F_SOOT), F_SOOT ** -0.5, 1.0, (), jnp.float32),
    }


HIGH = lax.Precision.HIGHEST


def growth(state, growth_weight, yield_weight):
    sections = growth_weight.shape[0]
    soot_part = state[:sections]
    species = state[sections:]
    growth_rate = jax.nn.sigmoid(jnp.dot(growth_weight, species, precision=HIGH, preferred_element_type=jnp.float32))
    section_flux = growth_rate * soot_part
    previous = jnp.concatenate([jnp.zeros_like(section_flux[:1]), section_flux[:-1]], axis=0)
    soot_next = soot_part + 0.5 * (previous - section_flux)
    species_next = species + 0.5 * jnp.dot(yield_weight, section_flux, precision=HIGH, preferred_element_type=jnp.float32)
    return jnp.concatenate([soot_next, species_next], axis=0)


def transport(field, params, inv_spacing):
    diffusivity, velocity, growth_weight, yield_weight = params
    centre = field[:, 1:-1, 1:-1, 1:-1]
    lower_z = field[:, :-2, 1:-1, 1:-1]
    lower_x = field[:, 1:-1, :-2, 1:-1]
    lower_y = field[:, 1:-1, 1:-1, :-2]
    neighbours = lower_z + field[:, 2:, 1:-1, 1:-1] + lower_x + field[:, 1:-1, 2:, 1:-1] + lower_y + field[:, 1:-1, 1:-1, 2:]
    laplace = neighbours - 6.0 * centre
    upwind = velocity[0] * (centre - lower_z) + velocity[1] * (centre - lower_x) + velocity[2] * (centre - lower_y)
    moved = centre + diffusivity[:, None, None, None] * (inv_spacing * inv_spacing) * laplace - inv_spacing * upwind
    shape = moved.shape
    return growth(moved.reshape(shape[0], -1), growth_weight, yield_weight).reshape(shape)


def interp_matrix(width):
    length = 2 * width - 4
    fine_index = jnp.arange(length)
    parent = fine_index // 2 + 1
    other_parent = parent + jnp.where(fine_index % 2 == 0, -1, 1)
    columns = jnp.arange(width)
    return (0.75 * (columns[None, :] == parent[:, None]) + 0.25 * (columns[None, :] == other_parent[:, None])).astype(jnp.float32)


def assemble(window, patch_cells):
    matrix = interp_matrix(window.shape[-1])
    result = jnp.einsum('fabc,ia->fibc', window, matrix, precision=HIGH)
    result = jnp.einsum('fibc,jb->fijc', result, matrix, precision=HIGH)
    result = jnp.einsum('fijc,kc->fijk', result, matrix, precision=HIGH)
    edge = result.shape[-1] - 4
    interior = patch_cells.astype(jnp.float32).reshape(result.shape[0], edge, edge, edge)
    return result.at[:, 2:-2, 2:-2, 2:-2].set(interior)


def advance_patch(ghosted, level, params):
    twice = transport(transport(ghosted, params, 1.0), params, 1.0)
    once = transport(ghosted[:, 1:-1, 1:-1, 1:-1], params, 1.0)
    return jnp.where(level == 2, twice, once)


def reference(coarse, fine_patches, new_owner, corners, level_tags, diffusivity, velocity, growth_weight, yield_weight):
    params = (diffusivity, velocity, growth_weight, yield_weight)
    padded = jnp.pad(coarse, ((0, 0), (2, 2), (2, 2), (2, 2)))
    coarse_next = transport(padded[:, 1:-1, 1:-1, 1:-1], params, 0.5)
    devices = N_REGION * N_PATCH
    device_id = jnp.arange(devices)
    region_of = device_id // N_PATCH
    column_of = device_id % N_PATCH
    corner_grid = corners.reshape(devices, P_DEV, 3)
    starts = jnp.stack([region_of[:, None] * CZ + corner_grid[:, :, 0], column_of[:, None] * CX + corner_grid[:, :, 1], corner_grid[:, :, 2]], axis=-1).astype(jnp.int32)
    width = B // 2 + 4

    def one_patch(start, patch_cells, level):
        window = lax.dynamic_slice(padded, (jnp.int32(0), start[0], start[1], start[2]), (FIELDS, width, width, width))
        result = advance_patch(assemble(window, patch_cells), level, params)
        return result.reshape(FIELDS, -1).astype(jnp.bfloat16)

    def one_device(inputs):
        start_rows, cell_rows, level_rows = inputs
        return jax.vmap(one_patch)(start_rows, cell_rows, level_rows)

    advanced = lax.map(one_device, (starts, fine_patches.reshape(devices, P_DEV, FIELDS, -1), level_tags.reshape(devices, P_DEV)))
    per_region = N_PATCH * P_DEV
    owners = new_owner.reshape(N_REGION, per_region)
    same = owners[:, :, None] == owners[:, None, :]
    earlier = jnp.arange(per_region)[None, :] < jnp.arange(per_region)[:, None]
    offsets = jnp.sum(jnp.logical_and(same, earlier[None]), axis=2)
    slot = (jnp.arange(N_REGION)[:, None] * N_PATCH + owners) * RECV + offsets
    fine_next = jnp.zeros((SLOTS, FIELDS, B ** 3), jnp.bfloat16).at[slot.reshape(-1).astype(jnp.int32)].set(advanced.reshape(-1, FIELDS, B ** 3))
    return coarse_next, fine_next
```

```python
import functools

import jax
import jax.numpy as jnp
import numpy as np
from jax import lax
from jax.experimental import pallas as pl
from jax.experimental.pallas import tpu as pltpu
from jax.sharding import PartitionSpec as P

B = 16
SOOT = 40
SPEC = 30
FIELDS = 70
ROWS = 72
WIN = 12
EDGE = 20
LANES = 384
WIDE = 512
NY = 128
PLANES = 16
PEERS = 16
UNIT = 144
MESH = pl.DeviceIdType.MESH
F32 = jnp.float32
BF16 = jnp.bfloat16


def spread_matrix():
    e = np.zeros((B * B, WIDE), np.float32)
    for x in range(B):
        for y in range(B):
            e[x * B + y, (x + 2) * EDGE + y + 2] = 1.0
    return e


def interp_weights():
    m = np.zeros((EDGE, WIN), np.float32)
    for f in range(EDGE):
        parent = f // 2 + 1
        m[f, parent] = 0.75
        m[f, parent + (-1 if f % 2 == 0 else 1)] = 0.25
    v = np.zeros((256, WIDE), np.float32)
    for x in range(WIN):
        for y in range(WIN):
            v[16 * x + y, : EDGE * EDGE] = np.outer(m[:, x], m[:, y]).reshape(-1)
    return v


def dot(a, b):
    return lax.dot_general(a, b, (((1,), (0,)), ((), ())), preferred_element_type=F32)


def pack_pair(a, b):
    return jnp.concatenate([a[:64], b[:64], a[64:ROWS], b[64:ROWS]], axis=0).astype(BF16)


def unpack_pair(u):
    u = u.astype(F32)
    first = jnp.concatenate([u[:64], u[128:136]], axis=0)
    second = jnp.concatenate([u[64:128], u[136:144]], axis=0)
    return first, second


def growth(moved, gw, aw):
    soot = moved[:SOOT]
    spec = moved[SOOT:]
    sh = spec.astype(BF16)
    sl = (spec - sh.astype(F32)).astype(BF16)
    pre = dot(gw, jnp.concatenate([sh, sl, sh], axis=0))
    rate = 0.5 * jnp.tanh(0.5 * pre) + 0.5
    flux = rate * soot
    fh = flux.astype(BF16).astype(F32)
    fl = flux - fh
    return moved + dot(aw, jnp.concatenate([fh, fl, fh], axis=0).astype(BF16))


def tiled(a, n):
    return jnp.concatenate([a] * n, axis=1)


def moved_terms(c, lz, uz, lx, ux, ly, uy, own, diff, v):
    total = (lz + uz) + (lx + ux) + (ly + uy)
    return own * c + diff * total + (v[0] * lz + v[1] * lx + v[2] * ly)


def load_rows(coarse_vmem, z, x):
    return coarse_vmem[pl.ds(z * 8 + x, ROWS, stride=64), :]


def stage_coarse(coarse_hbm, coarse_vmem, sem):
    copy = pltpu.make_async_copy(coarse_hbm, coarse_vmem.at[pl.ds(0, FIELDS * 64)], sem)
    copy.start()
    coarse_vmem[FIELDS * 64 :, :] = jnp.zeros((ROWS * 64 - FIELDS * 64, NY), F32)
    return copy


def halo_kernel(coarse_hbm, got, coarse_vmem, units, in_sem, send_sem, recv_sem):
    r, p = lax.axis_index("region"), lax.axis_index("patch")
    nr, np_ = lax.axis_size("region"), lax.axis_size("patch")
    up_r, down_r = lax.rem(r + 1, nr), lax.rem(r + nr - 1, nr)
    up_p, down_p = lax.rem(p + 1, np_), lax.rem(p + np_ - 1, np_)
    sends = [
        ((up_r, p), 8, 8, 0),
        ((down_r, p), 0, 8, 8),
        ((r, up_p), 24, 8, 16),
        ((r, down_p), 16, 8, 24),
        ((up_r, up_p), 14, 2, 32),
        ((up_r, down_p), 8, 2, 34),
        ((down_r, up_p), 6, 2, 36),
        ((down_r, down_p), 0, 2, 38),
    ]
    barrier = pltpu.get_barrier_semaphore()
    for device, _, _, _ in sends:
        pl.semaphore_signal(barrier, inc=1, device_id=device, device_id_type=MESH)
    stage_coarse(coarse_hbm, coarse_vmem, in_sem).wait()

    def fill(i, _):
        units[i] = pack_pair(load_rows(coarse_vmem, 0, i), load_rows(coarse_vmem, 1, i))
        units[8 + i] = pack_pair(load_rows(coarse_vmem, 6, i), load_rows(coarse_vmem, 7, i))
        units[16 + i] = pack_pair(load_rows(coarse_vmem, i, 0), load_rows(coarse_vmem, i, 1))
        units[24 + i] = pack_pair(load_rows(coarse_vmem, i, 6), load_rows(coarse_vmem, i, 7))
        return 0

    lax.fori_loop(0, 8, fill, 0)
    pl.semaphore_wait(barrier, 8)
    copies = []
    for n, (device, src, count, dst) in enumerate(sends):
        copy = pltpu.make_async_remote_copy(
            src_ref=units.at[pl.ds(src, count)],
            dst_ref=got.at[pl.ds(dst, count)],
            send_sem=send_sem.at[n],
            recv_sem=recv_sem.at[n],
            device_id=device,
            device_id_type=MESH,
        )
        copy.start()
        copies.append(copy)
    for copy in copies:
        copy.wait()


def halo(coarse):
    return pl.pallas_call(
        halo_kernel,
        out_shape=jax.ShapeDtypeStruct((40, UNIT, NY), BF16),
        in_specs=[pl.BlockSpec(memory_space=pl.ANY)],
        out_specs=pl.BlockSpec(memory_space=pltpu.VMEM),
        scratch_shapes=[
            pltpu.VMEM((ROWS * 64, NY), F32),
            pltpu.VMEM((32, UNIT, NY), BF16),
            pltpu.SemaphoreType.DMA,
            pltpu.SemaphoreType.DMA((8,)),
            pltpu.SemaphoreType.DMA((8,)),
        ],
        compiler_params=pltpu.CompilerParams(
            collective_id=0, has_side_effects=True, vmem_limit_bytes=32 * 1024 * 1024
        ),
        name="halo",
    )(coarse)


def fill_rows(coarse_vmem, got, rows, edges):
    z_low, z_high, x_low, x_high = edges

    def own(z, _):
        for x in range(8):
            rows[z + 2, :, pl.ds((x + 2) * NY, NY)] = load_rows(coarse_vmem, z, x)
        a, b = unpack_pair(got[16 + z])
        rows[z + 2, :, pl.ds(0, NY)] = a * x_low
        rows[z + 2, :, pl.ds(NY, NY)] = b * x_low
        a, b = unpack_pair(got[24 + z])
        rows[z + 2, :, pl.ds(10 * NY, NY)] = a * x_high
        rows[z + 2, :, pl.ds(11 * NY, NY)] = b * x_high
        return 0

    lax.fori_loop(0, 8, own, 0)
    for x in range(WIN):
        if x < 2:
            low, high, side = 32 + x, 36 + x, x_low
        elif x < 10:
            low, high, side = x - 2, 8 + x - 2, 1.0
        else:
            low, high, side = 34 + x - 10, 38 + x - 10, x_high
        for unit, z, scale in ((low, 0, z_low * side), (high, 10, z_high * side)):
            a, b = unpack_pair(got[unit])
            rows[z, :, pl.ds(x * NY, NY)] = a * scale
            rows[z + 1, :, pl.ds(x * NY, NY)] = b * scale


def advance_coarse(rows, out, coef, vel, gw, aw):
    width = 4 * NY
    lane = lax.broadcasted_iota(jnp.int32, (ROWS, width), 1) % NY

    def step(i, _):
        z = i // 2 + 2
        base = pl.multiple_of((i % 2) * width, width)

        def part(dz, dx):
            return rows[z + dz, :, pl.ds(pl.multiple_of(base + (2 + dx) * NY, NY), width)]

        c = part(0, 0)
        pieces = [c[:, n * NY : (n + 1) * NY] for n in range(4)]
        ly = jnp.concatenate([pltpu.roll(t, 1, 1) for t in pieces], axis=1)
        uy = jnp.concatenate([pltpu.roll(t, NY - 1, 1) for t in pieces], axis=1)
        ly = jnp.where(lane == 0, 0.0, ly)
        uy = jnp.where(lane == NY - 1, 0.0, uy)
        moved = moved_terms(
            c, part(-1, 0), part(1, 0), part(0, -1), part(0, 1), ly, uy,
            tiled(coef[2], 4), tiled(coef[3], 4), (vel[3], vel[4], vel[5]),
        )
        new = growth(moved, gw, aw)
        for n in range(4):
            at = (z - 2) * 8 + (i % 2) * 4 + n
            out[pl.ds(at, FIELDS, stride=64), :] = new[:FIELDS, n * NY : (n + 1) * NY]
        return 0

    lax.fori_loop(0, 16, step, 0)


def build_windows(rows, corner, picks, window, weights):
    lane = lax.broadcasted_iota(jnp.int32, (NY, 256), 1)
    row = lax.broadcasted_iota(jnp.int32, (NY, 256), 0)
    start = jnp.where(lane < NY, corner[0], corner[1]) - 2
    slot = lane % NY
    for x in range(8):
        at = slot - 16 * x
        hit = jnp.logical_and(jnp.logical_and(at >= 0, at < WIN), row == start + at)
        picks[pl.ds(x * NY, NY), :] = jnp.where(hit, 1.0, 0.0).astype(BF16)
    v = weights[...]

    def group(g, _):
        z = g * 3
        lhs = rows[pl.ds(z, 3)].reshape(3 * ROWS, WIN * NY).astype(BF16)
        first = dot(lhs[:, : 8 * NY], picks[...]).astype(BF16)
        second = dot(lhs[:, 8 * NY :], picks[: 4 * NY, :]).astype(BF16)
        for n in range(2):
            cut = slice(n * NY, (n + 1) * NY)
            both = jnp.concatenate([first[:, cut], second[:, cut]], axis=1)
            window[n, pl.ds(z, 3)] = dot(both, v).reshape(3, ROWS, WIDE)
        return 0

    lax.fori_loop(0, 4, group, 0)


def build_ghosted(window, cells, ghosted, spread):
    lane = lax.broadcasted_iota(jnp.int32, (ROWS, WIDE), 1)
    x, y = lane // EDGE, lane % EDGE
    inside = (x >= 2) & (x < 18) & (y >= 2) & (y < 18)
    e = spread[...]
    pad = jnp.zeros((ROWS - FIELDS, 256), F32)

    def blend(n, f, parent, other):
        return 0.75 * window[n, parent] + 0.25 * window[n, other]

    for n in range(2):
        for f in (0, 1, 18, 19):
            parent = f // 2 + 1
            ghosted[n, f] = blend(n, f, parent, parent + (-1 if f % 2 == 0 else 1))

    def group(g, _):
        for n in range(2):
            planes = []
            for k in range(4):
                at = pl.multiple_of((g * 4 + k) * 256, 256)
                planes.append(jnp.concatenate([cells[n, :, pl.ds(at, 256)].astype(F32), pad], axis=0))
            full = dot(jnp.concatenate(planes, axis=0).astype(BF16), e)
            for k in range(4):
                f = 2 + g * 4 + k
                parent = 2 + g * 2 + k // 2
                other = parent + (-1 if k % 2 == 0 else 1)
                ghosted[n, f] = jnp.where(inside, full[k * ROWS : (k + 1) * ROWS], blend(n, f, parent, other))
        return 0

    lax.fori_loop(0, 4, group, 0)


def first_step(ghosted, z, coef, vel, gw, aw):
    moved = []
    for n in range(2):
        wide = ghosted[n, z]
        c = wide[:, :LANES]
        moved.append(
            moved_terms(
                c,
                ghosted[n, z - 1, :, :LANES],
                ghosted[n, z + 1, :, :LANES],
                pltpu.roll(c, EDGE, 1),
                pltpu.roll(wide, WIDE - EDGE, 1)[:, :LANES],
                pltpu.roll(c, 1, 1),
                pltpu.roll(c, LANES - 1, 1),
                tiled(coef[0], 3), tiled(coef[1], 3), (vel[0], vel[1], vel[2]),
            )
        )
    return growth(jnp.concatenate(moved, axis=1), gw, aw)


def second_step(once, z, coef, vel, gw, aw):
    moved = []
    for n in range(2):
        cut = pl.ds(n * LANES, LANES)
        c = once[z, :, cut]
        moved.append(
            moved_terms(
                c,
                once[z - 1, :, cut],
                once[z + 1, :, cut],
                pltpu.roll(c, EDGE, 1),
                pltpu.roll(c, LANES - EDGE, 1),
                pltpu.roll(c, 1, 1),
                pltpu.roll(c, LANES - 1, 1),
                tiled(coef[0], 3), tiled(coef[1], 3), (vel[0], vel[1], vel[2]),
            )
        )
    return growth(jnp.concatenate(moved, axis=1), gw, aw)


def advance_kernel(
    corner, level, vel, coarse_hbm, got, cells, coef, gw_ref, aw_ref, spread, gather, weights,
    coarse_out, packed, coarse_vmem, rows, picks, window, ghosted, once, sem,
):
    r, p = lax.axis_index("region"), lax.axis_index("patch")
    nr, np_ = lax.axis_size("region"), lax.axis_size("patch")
    edges = [jnp.where(hit, 0.0, 1.0) for hit in (r == 0, r == nr - 1, p == 0, p == np_ - 1)]
    stage_coarse(coarse_hbm, coarse_vmem, sem).wait()
    fill_rows(coarse_vmem, got, rows, edges)
    gw, aw = gw_ref[...], aw_ref[...]
    build_windows(rows, corner, picks, window, weights)
    build_ghosted(window, cells, ghosted, spread)
    lane = lax.broadcasted_iota(jnp.int32, (ROWS, 2 * LANES), 1)
    twice = jnp.where(lane < LANES, level[0], level[1]) == 2
    for z in (1, 2, 3):
        once[z] = first_step(ghosted, z, coef, vel, gw, aw)

    def plane(z, _):
        second = second_step(once, z, coef, vel, gw, aw)
        chosen = jnp.where(twice, second, once[z]).astype(BF16)
        ahead = jnp.minimum(z + 2, 18)
        once[ahead] = first_step(ghosted, ahead, coef, vel, gw, aw)
        pair = [dot(chosen[:, n * LANES : (n + 1) * LANES], gather[...]) for n in range(2)]
        packed[z - 2] = pack_pair(*pair)
        return 0

    lax.fori_loop(2, 18, plane, 0)
    advance_coarse(rows, coarse_out, coef, vel, gw, aw)


def advance(corner, level, vel, coarse, got, cells, coef, gw, aw):
    spread = jnp.asarray(spread_matrix(), BF16)
    gather = jnp.asarray(spread_matrix()[:, :LANES].T.copy(), BF16)
    weights = jnp.asarray(interp_weights(), BF16)
    vmem = pl.BlockSpec(memory_space=pltpu.VMEM)
    smem = pl.BlockSpec(memory_space=pltpu.SMEM)
    return pl.pallas_call(
        advance_kernel,
        out_shape=(
            jax.ShapeDtypeStruct((FIELDS * 64, NY), F32),
            jax.ShapeDtypeStruct((PLANES, UNIT, 256), BF16),
        ),
        in_specs=[smem, smem, smem, pl.BlockSpec(memory_space=pl.ANY)] + [vmem] * 8,
        out_specs=(vmem, vmem),
        scratch_shapes=[
            pltpu.VMEM((ROWS * 64, NY), F32),
            pltpu.VMEM((WIN, ROWS, WIN * NY), F32),
            pltpu.VMEM((8 * NY, 256), BF16),
            pltpu.VMEM((2, WIN, ROWS, WIDE), F32),
            pltpu.VMEM((2, EDGE, ROWS, WIDE), F32),
            pltpu.VMEM((EDGE, ROWS, 2 * LANES), F32),
            pltpu.SemaphoreType.DMA,
        ],
        compiler_params=pltpu.CompilerParams(vmem_limit_bytes=56 * 1024 * 1024),
        name="advance",
    )(corner, level, vel, coarse, got, cells, coef, gw, aw, spread, gather, weights)


def exchange_kernel(pick, keep, packed, landed, spread_in, staged, s1, r1, s2, r2):
    r, p = lax.axis_index("region"), lax.axis_index("patch")
    barrier = pltpu.get_barrier_semaphore()
    for d in range(1, PEERS):
        pl.semaphore_signal(
            barrier, inc=1, device_id=(r, lax.rem(p + d, PEERS)), device_id_type=MESH
        )
    pl.semaphore_wait(barrier, PEERS - 1)

    def first(d):
        peer = lax.rem(p + d, PEERS)
        return pltpu.make_async_remote_copy(
            src_ref=packed.at[peer],
            dst_ref=spread_in.at[p],
            send_sem=s1.at[d],
            recv_sem=r1.at[d],
            device_id=(r, peer),
            device_id_type=MESH,
        )

    def second(d):
        return pltpu.make_async_remote_copy(
            src_ref=staged.at[d],
            dst_ref=landed.at[p],
            send_sem=s2.at[d],
            recv_sem=r2.at[d],
            device_id=(r, lax.rem(p + d, PEERS)),
            device_id_type=MESH,
        )

    def each(body):
        lax.fori_loop(1, PEERS, lambda d, _: (body(d), 0)[1], 0)

    each(lambda d: first(d).start())
    spread_in[p] = packed[p]
    each(lambda d: first(d).wait())

    def item(owner, k):
        n = owner * 2 + k
        chunk = spread_in[pick[n]]
        return jnp.where(keep[n] > 0, chunk, jnp.zeros_like(chunk))

    def send(d):
        owner = lax.rem(p + d, PEERS)
        for k in range(2):
            staged[d, k] = item(owner, k)
        second(d).start()

    each(send)
    for k in range(2):
        landed[p, k] = item(p, k)
    each(lambda d: second(d).wait())


def exchange(pick, keep, packed):
    vmem = pl.BlockSpec(memory_space=pltpu.VMEM)
    smem = pl.BlockSpec(memory_space=pltpu.SMEM)
    return pl.pallas_call(
        exchange_kernel,
        out_shape=jax.ShapeDtypeStruct((PEERS, 2, UNIT, 256), BF16),
        in_specs=[smem, smem, vmem],
        out_specs=vmem,
        scratch_shapes=[
            pltpu.VMEM((PEERS, UNIT, 256), BF16),
            pltpu.VMEM((PEERS, 2, UNIT, 256), BF16),
        ]
        + [pltpu.SemaphoreType.DMA((PEERS,))] * 4,
        compiler_params=pltpu.CompilerParams(
            collective_id=1, has_side_effects=True, vmem_limit_bytes=32 * 1024 * 1024
        ),
        name="exchange",
    )(pick, keep, packed)


def place_kernel(landed, out):
    for j in range(PLANES):
        first, second = unpack_pair(landed[j, 0])
        out[0, :, pl.ds(j * 256, 256)] = first[:FIELDS].astype(BF16)
        out[1, :, pl.ds(j * 256, 256)] = second[:FIELDS].astype(BF16)


def place(landed):
    return pl.pallas_call(
        place_kernel,
        grid=(2,),
        out_shape=jax.ShapeDtypeStruct((4, FIELDS, B**3), BF16),
        in_specs=[pl.BlockSpec((PLANES, 1, UNIT, 256), lambda k: (0, k, 0, 0))],
        out_specs=pl.BlockSpec((2, FIELDS, B**3), lambda k: (k, 0, 0)),
        name="place",
    )(landed)


def split(x):
    high = lax.reduce_precision(x, 8, 7)
    return high, x - high


def parameters(diffusivity, velocity, growth_weight, yield_weight):
    flow = jnp.sum(velocity)
    d = jnp.pad(diffusivity, (0, ROWS - FIELDS))
    columns = jnp.stack([1.0 - 6.0 * d - flow, d, 1.0 - 1.5 * d - 0.5 * flow, 0.25 * d])
    coef = jnp.broadcast_to(columns[:, :, None], (4, ROWS, NY))
    vel = jnp.concatenate([velocity, 0.5 * velocity])
    gh, gl = split(jnp.pad(growth_weight, ((0, 0), (0, 32 - SPEC))))
    gw = jnp.concatenate([gh, gh, gl], axis=1).astype(BF16)
    change = jnp.eye(SOOT, k=-1, dtype=F32) - jnp.eye(SOOT, dtype=F32)
    both = 0.5 * jnp.concatenate([change, yield_weight, jnp.zeros((ROWS - FIELDS, SOOT), F32)])
    ah, al = split(both)
    aw = jnp.concatenate([ah, ah, al], axis=1).astype(BF16)
    return coef, vel, gw, aw


def shards(
    coarse, fine_patches, new_owner, corners, level_tags, diffusivity, velocity, growth_weight, yield_weight
):
    owners = lax.all_gather(new_owner[:1, 0], "patch", tiled=True)
    before = jnp.arange(PEERS)[None, :] < jnp.arange(PEERS)[:, None]
    rank = jnp.sum((owners[:, None] == owners[None, :]) & before, axis=1)
    slot = owners * 2 + rank
    match = slot[None, :] == jnp.arange(2 * PEERS)[:, None]
    pick = jnp.sum(jnp.where(match, jnp.arange(PEERS)[None, :], 0), axis=1)
    keep = jnp.any(match, axis=1).astype(jnp.int32)
    coef, vel, gw, aw = parameters(diffusivity, velocity, growth_weight, yield_weight)
    flat = coarse.reshape(FIELDS * 64, NY)
    got = halo(flat)
    coarse_next, packed = advance(corners[:, 2], level_tags, vel, flat, got, fine_patches, coef, gw, aw)
    landed = exchange(pick, keep, packed)
    return coarse_next.reshape(coarse.shape), place(landed)


def solution(mesh):
    placed = (
        P(None, "region", "patch", None),
        P(("region", "patch"), None, None),
        P(("region", "patch"), None),
        P(("region", "patch"), None),
        P(("region", "patch")),
        P(),
        P(),
        P(),
        P(),
    )
    return jax.shard_map(
        shards,
        mesh=mesh,
        in_specs=placed,
        out_specs=(P(None, "region", "patch", None), P(("region", "patch"), None, None)),
        check_vma=False,
    )
```

```python
import functools

import jax
import jax.numpy as jnp
import numpy as np
from jax import lax
from jax.experimental import pallas as pl
from jax.experimental.pallas import tpu as pltpu
from jax.sharding import PartitionSpec as P

B = 16
SOOT = 40
SPEC = 30
FIELDS = 70
ROWS = 72
WIN = 12
EDGE = 20
LANES = 384
WIDE = 512
NY = 128
PLANES = 16
PEERS = 16
UNIT = 144
MESH = pl.DeviceIdType.MESH
F32 = jnp.float32
BF16 = jnp.bfloat16


def spread_matrix():
    e = np.zeros((B * B, WIDE), np.float32)
    for x in range(B):
        for y in range(B):
            e[x * B + y, (x + 2) * EDGE + y + 2] = 1.0
    return e


def interp_weights():
    m = np.zeros((EDGE, WIN), np.float32)
    for f in range(EDGE):
        parent = f // 2 + 1
        m[f, parent] = 0.75
        m[f, parent + (-1 if f % 2 == 0 else 1)] = 0.25
    v = np.zeros((256, WIDE), np.float32)
    for x in range(WIN):
        for y in range(WIN):
            v[16 * x + y, : EDGE * EDGE] = np.outer(m[:, x], m[:, y]).reshape(-1)
    return v


def dot(a, b):
    return lax.dot_general(a, b, (((1,), (0,)), ((), ())), preferred_element_type=F32)


def pack_pair(a, b):
    return jnp.concatenate([a[:64], b[:64], a[64:ROWS], b[64:ROWS]], axis=0).astype(BF16)


def unpack_pair(u):
    u = u.astype(F32)
    first = jnp.concatenate([u[:64], u[128:136]], axis=0)
    second = jnp.concatenate([u[64:128], u[136:144]], axis=0)
    return first, second


def growth(moved, gw, aw):
    soot = moved[:SOOT]
    spec = moved[SOOT:]
    sh = spec.astype(BF16)
    sl = (spec - sh.astype(F32)).astype(BF16)
    pre = dot(gw, jnp.concatenate([sh, sl, sh], axis=0))
    rate = 0.5 * jnp.tanh(0.5 * pre) + 0.5
    flux = rate * soot
    fh = flux.astype(BF16).astype(F32)
    fl = flux - fh
    return moved + dot(aw, jnp.concatenate([fh, fl, fh], axis=0).astype(BF16))


def tiled(a, n):
    return jnp.concatenate([a] * n, axis=1)


def moved_terms(c, lz, uz, lx, ux, ly, uy, own, diff, v):
    total = (lz + uz) + (lx + ux) + (ly + uy)
    return own * c + diff * total + (v[0] * lz + v[1] * lx + v[2] * ly)


def load_rows(coarse_vmem, z, x):
    return coarse_vmem[pl.ds(z * 8 + x, ROWS, stride=64), :]


def stage_coarse(coarse_hbm, coarse_vmem, sem):
    copy = pltpu.make_async_copy(coarse_hbm, coarse_vmem.at[pl.ds(0, FIELDS * 64)], sem)
    copy.start()
    coarse_vmem[FIELDS * 64 :, :] = jnp.zeros((ROWS * 64 - FIELDS * 64, NY), F32)
    return copy


def fill_rows(coarse_vmem, got, rows, edges):
    z_low, z_high, x_low, x_high = edges

    def own(z, _):
        for x in range(8):
            rows[z + 2, :, pl.ds((x + 2) * NY, NY)] = load_rows(coarse_vmem, z, x)
        a, b = unpack_pair(got[16 + z])
        rows[z + 2, :, pl.ds(0, NY)] = a * x_low
        rows[z + 2, :, pl.ds(NY, NY)] = b * x_low
        a, b = unpack_pair(got[24 + z])
        rows[z + 2, :, pl.ds(10 * NY, NY)] = a * x_high
        rows[z + 2, :, pl.ds(11 * NY, NY)] = b * x_high
        return 0

    lax.fori_loop(0, 8, own, 0)
    for x in range(WIN):
        if x < 2:
            low, high, side = 32 + x, 36 + x, x_low
        elif x < 10:
            low, high, side = x - 2, 8 + x - 2, 1.0
        else:
            low, high, side = 34 + x - 10, 38 + x - 10, x_high
        for unit, z, scale in ((low, 0, z_low * side), (high, 10, z_high * side)):
            a, b = unpack_pair(got[unit])
            rows[z, :, pl.ds(x * NY, NY)] = a * scale
            rows[z + 1, :, pl.ds(x * NY, NY)] = b * scale


def advance_coarse(rows, out, coef, vel, gw, aw, first):
    width = 4 * NY
    lane = lax.broadcasted_iota(jnp.int32, (ROWS, width), 1) % NY

    def step(i, _):
        z = i // 2 + 2
        base = pl.multiple_of((i % 2) * width, width)

        def part(dz, dx):
            return rows[z + dz, :, pl.ds(pl.multiple_of(base + (2 + dx) * NY, NY), width)]

        c = part(0, 0)
        pieces = [c[:, n * NY : (n + 1) * NY] for n in range(4)]
        ly = jnp.concatenate([pltpu.roll(t, 1, 1) for t in pieces], axis=1)
        uy = jnp.concatenate([pltpu.roll(t, NY - 1, 1) for t in pieces], axis=1)
        ly = jnp.where(lane == 0, 0.0, ly)
        uy = jnp.where(lane == NY - 1, 0.0, uy)
        moved = moved_terms(
            c, part(-1, 0), part(1, 0), part(0, -1), part(0, 1), ly, uy,
            tiled(coef[2], 4), tiled(coef[3], 4), (vel[3], vel[4], vel[5]),
        )
        new = growth(moved, gw, aw)
        for n in range(4):
            at = (z - 2) * 8 + (i % 2) * 4 + n
            out[pl.ds(at, FIELDS, stride=64), :] = new[:FIELDS, n * NY : (n + 1) * NY]
        return 0

    lax.fori_loop(first, first + 8, step, 0)


def build_windows(rows, corner, picks, window, weights):
    lane = lax.broadcasted_iota(jnp.int32, (NY, 256), 1)
    row = lax.broadcasted_iota(jnp.int32, (NY, 256), 0)
    start = jnp.where(lane < NY, corner[0], corner[1]) - 2
    slot = lane % NY
    for x in range(8):
        at = slot - 16 * x
        hit = jnp.logical_and(jnp.logical_and(at >= 0, at < WIN), row == start + at)
        picks[pl.ds(x * NY, NY), :] = jnp.where(hit, 1.0, 0.0).astype(BF16)
    v = weights[...]

    def group(g, _):
        z = g * 3
        lhs = rows[pl.ds(z, 3)].reshape(3 * ROWS, WIN * NY).astype(BF16)
        first = dot(lhs[:, : 8 * NY], picks[...]).astype(BF16)
        second = dot(lhs[:, 8 * NY :], picks[: 4 * NY, :]).astype(BF16)
        for n in range(2):
            cut = slice(n * NY, (n + 1) * NY)
            both = jnp.concatenate([first[:, cut], second[:, cut]], axis=1)
            window[n, pl.ds(z, 3)] = dot(both, v).reshape(3, ROWS, WIDE)
        return 0

    lax.fori_loop(0, 4, group, 0)


def build_ghosted(window, cells, ghosted, spread):
    lane = lax.broadcasted_iota(jnp.int32, (ROWS, WIDE), 1)
    x, y = lane // EDGE, lane % EDGE
    inside = (x >= 2) & (x < 18) & (y >= 2) & (y < 18)
    e = spread[...]
    pad = jnp.zeros((ROWS - FIELDS, 256), F32)

    def blend(n, f, parent, other):
        return 0.75 * window[n, parent] + 0.25 * window[n, other]

    for n in range(2):
        for f in (0, 1, 18, 19):
            parent = f // 2 + 1
            ghosted[n, f] = blend(n, f, parent, parent + (-1 if f % 2 == 0 else 1))

    def group(g, _):
        for n in range(2):
            planes = []
            for k in range(4):
                at = pl.multiple_of((g * 4 + k) * 256, 256)
                planes.append(jnp.concatenate([cells[n, :, pl.ds(at, 256)].astype(F32), pad], axis=0))
            full = dot(jnp.concatenate(planes, axis=0).astype(BF16), e)
            for k in range(4):
                f = 2 + g * 4 + k
                parent = 2 + g * 2 + k // 2
                other = parent + (-1 if k % 2 == 0 else 1)
                ghosted[n, f] = jnp.where(inside, full[k * ROWS : (k + 1) * ROWS], blend(n, f, parent, other))
        return 0

    lax.fori_loop(0, 4, group, 0)


def first_step(ghosted, z, coef, vel, gw, aw):
    moved = []
    for n in range(2):
        wide = ghosted[n, z]
        c = wide[:, :LANES]
        moved.append(
            moved_terms(
                c,
                ghosted[n, z - 1, :, :LANES],
                ghosted[n, z + 1, :, :LANES],
                pltpu.roll(c, EDGE, 1),
                pltpu.roll(wide, WIDE - EDGE, 1)[:, :LANES],
                pltpu.roll(c, 1, 1),
                pltpu.roll(c, LANES - 1, 1),
                tiled(coef[0], 3), tiled(coef[1], 3), (vel[0], vel[1], vel[2]),
            )
        )
    return growth(jnp.concatenate(moved, axis=1), gw, aw)


def second_step(once, z, coef, vel, gw, aw):
    moved = []
    for n in range(2):
        cut = pl.ds(n * LANES, LANES)
        c = once[z, :, cut]
        moved.append(
            moved_terms(
                c,
                once[z - 1, :, cut],
                once[z + 1, :, cut],
                pltpu.roll(c, EDGE, 1),
                pltpu.roll(c, LANES - EDGE, 1),
                pltpu.roll(c, 1, 1),
                pltpu.roll(c, LANES - 1, 1),
                tiled(coef[0], 3), tiled(coef[1], 3), (vel[0], vel[1], vel[2]),
            )
        )
    return growth(jnp.concatenate(moved, axis=1), gw, aw)


def remote(src, dst, send, recv, device):
    return pltpu.make_async_remote_copy(
        src_ref=src, dst_ref=dst, send_sem=send, recv_sem=recv, device_id=device, device_id_type=MESH
    )


def mod4(a):
    return lax.rem(a + 8, 4)


def loop(start, stop, body):
    lax.fori_loop(start, stop, lambda i, _: (body(i), 0)[1], 0)


def fused_kernel(
    corner, level, vel, owner, coarse_hbm, cells, coef, gw_ref, aw_ref, spread, gather, weights,
    coarse_out, landed,
    coarse_vmem, rows, picks, window, ghosted, once,
    units, got, row_tiles, tiles, order, order_smem,
    packed, mid0, mid1, held0, held1, staged0, staged1, relay0, relay1,
    load_sem, halo_s, halo_r, tile_s, tile_r, s1a, r1a, s1b, r1b, s2a, r2a, s2b, r2b, s3a, r3a, s3b, r3b, s4a, r4a, s4b, r4b,
):
    r, p = lax.axis_index("region"), lax.axis_index("patch")
    nr, np_ = lax.axis_size("region"), lax.axis_size("patch")
    y, x = p // 4, lax.rem(p, 4)
    up_r, down_r = lax.rem(r + 1, nr), lax.rem(r + nr - 1, nr)
    up_p, down_p = lax.rem(p + 1, np_), lax.rem(p + np_ - 1, np_)
    mine = mod4(y - x)

    def at(yy, xx):
        return (r, yy * 4 + xx)

    halo_sends = [
        ((up_r, p), 8, 8, 0),
        ((down_r, p), 0, 8, 8),
        ((r, up_p), 24, 8, 16),
        ((r, down_p), 16, 8, 24),
        ((up_r, up_p), 14, 2, 32),
        ((up_r, down_p), 8, 2, 34),
        ((down_r, up_p), 6, 2, 36),
        ((down_r, down_p), 0, 2, 38),
    ]
    barrier = pltpu.get_barrier_semaphore()
    for device, _, _, _ in halo_sends:
        pl.semaphore_signal(barrier, inc=1, device_id=device, device_id_type=MESH)
    for d in (1, 2, 3):
        pl.semaphore_signal(barrier, inc=1, device_id=at(y, mod4(x + d)), device_id_type=MESH)
        pl.semaphore_signal(barrier, inc=1, device_id=at(mod4(y + d), x), device_id_type=MESH)
    load = stage_coarse(coarse_hbm, coarse_vmem, load_sem)
    row_tiles[x] = jnp.full((8, NY), owner[0], jnp.int32)
    held0[16] = jnp.zeros((UNIT, NY), BF16)
    held1[16] = jnp.zeros((UNIT, NY), BF16)
    load.wait()

    def fill(i):
        units[i] = pack_pair(load_rows(coarse_vmem, 0, i), load_rows(coarse_vmem, 1, i))
        units[8 + i] = pack_pair(load_rows(coarse_vmem, 6, i), load_rows(coarse_vmem, 7, i))
        units[16 + i] = pack_pair(load_rows(coarse_vmem, i, 0), load_rows(coarse_vmem, i, 1))
        units[24 + i] = pack_pair(load_rows(coarse_vmem, i, 6), load_rows(coarse_vmem, i, 7))

    loop(0, 8, fill)
    pl.semaphore_wait(barrier, 14)
    halos = [
        remote(units.at[pl.ds(src, count)], got.at[pl.ds(dst, count)], halo_s.at[n], halo_r.at[n], device)
        for n, (device, src, count, dst) in enumerate(halo_sends)
    ]
    for copy in halos:
        copy.start()

    def row_tile(d, slot):
        return remote(row_tiles.at[slot], row_tiles.at[slot], tile_s.at[d], tile_r.at[d], at(y, mod4(x + d)))

    def column_tile(d, slot):
        return remote(row_tiles, tiles.at[slot], tile_s.at[3 + d], tile_r.at[3 + d], at(mod4(y + d), x))

    for d in (1, 2, 3):
        row_tile(d, x).start()
    for d in (1, 2, 3):
        row_tile(d, x).wait_send()
        row_tile(d, mod4(x - d)).wait_recv()
    for d in (1, 2, 3):
        column_tile(d, y).start()
    tiles[y] = row_tiles[...]
    for d in (1, 2, 3):
        column_tile(d, y).wait_send()
        column_tile(d, mod4(y - d)).wait_recv()
    lane = lax.broadcasted_iota(jnp.int32, (8, NY), 1)
    owners = [tiles[i // 4, i % 4] for i in range(PEERS)]
    pick0 = jnp.full((8, NY), 16, jnp.int32)
    pick1 = pick0
    for i in range(PEERS):
        slot = owners[i] * 2
        for j in range(i):
            slot = slot + jnp.where(owners[j] == owners[i], 1, 0)
        pick0 = jnp.where(slot == lane, i, pick0)
        pick1 = jnp.where(slot == lane, (i % 4) * 4 + i // 4, pick1)
    order[0] = pick0
    order[1] = pick1
    to_smem = pltpu.make_async_copy(order, order_smem, load_sem)
    to_smem.start()
    to_smem.wait()
    for copy in halos:
        copy.wait()

    edges = [jnp.where(hit, 0.0, 1.0) for hit in (r == 0, r == nr - 1, p == 0, p == np_ - 1)]
    fill_rows(coarse_vmem, got, rows, edges)
    gw, aw = gw_ref[...], aw_ref[...]
    build_windows(rows, corner, picks, window, weights)
    build_ghosted(window, cells, ghosted, spread)
    lane = lax.broadcasted_iota(jnp.int32, (ROWS, 2 * LANES), 1)
    twice = jnp.where(lane < LANES, level[0], level[1]) == 2
    for z in (1, 2, 3):
        once[z] = first_step(ghosted, z, coef, vel, gw, aw)

    def send1a(j, q, xj):
        return remote(packed.at[j, 0], mid0.at[q, x], s1a.at[j], r1a.at[q * 4 + x], at(y, xj))

    def send1b(j, q, yj):
        return remote(packed.at[j, 1], mid1.at[q, y], s1b.at[j], r1b.at[q * 4 + y], at(yj, x))

    def wait1a(q, sx):
        remote(packed.at[0, 0], mid0.at[q, sx], s1a.at[0], r1a.at[q * 4 + sx], at(y, sx)).wait_recv()

    def wait1b(q, sy):
        remote(packed.at[0, 1], mid1.at[q, sy], s1b.at[0], r1b.at[q * 4 + sy], at(sy, x)).wait_recv()

    def send2a(q, yj):
        return remote(mid0.at[q], held0.at[pl.ds(y * 4, 4)], s2a.at[q], r2a.at[y], at(yj, x))

    def send2b(q, xj):
        return remote(mid1.at[q], held1.at[pl.ds(x * 4, 4)], s2b.at[q], r2b.at[x], at(y, xj))

    def wait2a(sy):
        remote(mid0.at[0], held0.at[pl.ds(sy * 4, 4)], s2a.at[0], r2a.at[sy], at(sy, x)).wait_recv()

    def wait2b(sx):
        remote(mid1.at[0], held1.at[pl.ds(sx * 4, 4)], s2b.at[0], r2b.at[sx], at(y, sx)).wait_recv()

    def send3a(xo):
        return remote(staged0.at[xo], relay0.at[x], s3a.at[xo], r3a.at[x], at(y, xo))

    def send3b(yo):
        return remote(staged1.at[yo], relay1.at[y], s3b.at[yo], r3b.at[y], at(yo, x))

    def wait3a(sx):
        remote(staged0.at[0], relay0.at[sx], s3a.at[0], r3a.at[sx], at(y, sx)).wait_recv()

    def wait3b(sy):
        remote(staged1.at[0], relay1.at[sy], s3b.at[0], r3b.at[sy], at(sy, x)).wait_recv()

    def send4a(q, yo):
        sx = mod4(y - q)
        return remote(relay0.at[sx, yo], landed.at[q * 4 + sx, 0], s4a.at[q * 4 + yo], r4a.at[q * 4 + sx], at(yo, x))

    def send4b(q, xo):
        sy = mod4(x + q)
        return remote(relay1.at[sy, xo], landed.at[q * 4 + x, 1], s4b.at[q * 4 + xo], r4b.at[q * 4 + x], at(y, xo))

    def wait4a(j):
        remote(relay0.at[0, 0], landed.at[j, 0], s4a.at[0], r4a.at[j], at(y, mod4(x + 1))).wait_recv()

    def wait4b(j):
        remote(relay1.at[0, 0], landed.at[j, 1], s4b.at[0], r4b.at[j], at(mod4(y + 1), x)).wait_recv()

    def plane(q, i):
        j = q * 4 + i
        z = j + 2
        second = second_step(once, z, coef, vel, gw, aw)
        chosen = jnp.where(twice, second, once[z]).astype(BF16)
        ahead = jnp.minimum(z + 2, 18)
        once[ahead] = first_step(ghosted, ahead, coef, vel, gw, aw)
        pair = [dot(chosen[:, n * LANES : (n + 1) * LANES], gather[...]) for n in range(2)]
        chunk = pack_pair(*pair)
        packed[j, 0] = chunk[:, :NY]
        packed[j, 1] = chunk[:, NY:]
        yj = mod4(i + q)

        @pl.when(i == x)
        def _():
            mid0[q, x] = packed[j, 0]

        @pl.when(i != x)
        def _():
            send1a(j, q, i).start()

        @pl.when(yj == y)
        def _():
            mid1[q, y] = packed[j, 1]

        @pl.when(yj != y)
        def _():
            send1b(j, q, yj).start()

    def forward(q):
        for d in (1, 2, 3):
            wait1a(q, mod4(x + d))
            wait1b(q, mod4(y + d))

        @pl.when(q == mine)
        def _():
            held0[pl.ds(y * 4, 4)] = mid0[q]
            held1[pl.ds(x * 4, 4)] = mid1[q]

        @pl.when(q != mine)
        def _():
            send2a(q, mod4(x + q)).start()
            send2b(q, mod4(y - q)).start()

    def deal():
        for d in (1, 2, 3):
            wait2a(mod4(y + d))
            wait2b(mod4(x + d))

        def one(d):
            xo, yo = mod4(x + d), mod4(y + d)

            def copy(n):
                k, other = lax.rem(n, 2), n // 2
                staged0[xo, other, k] = held0[order_smem[0, 0, (other * 4 + xo) * 2 + k]]
                staged1[yo, other, k] = held1[order_smem[1, 0, (yo * 4 + other) * 2 + k]]

            loop(0, 8, copy)

            @pl.when(d > 0)
            def _():
                send3a(xo).start()
                send3b(yo).start()

        loop(1, 4, one)
        one(0)
        relay0[x] = staged0[x]
        relay1[y] = staged1[y]

    def finish(q):
        sx, sy = mod4(y - q), mod4(x + q)

        @pl.when(q != mine)
        def _():
            wait3a(sx)
            wait3b(sy)

        for d in (1, 2, 3):
            send4a(q, mod4(y + d)).start()
            send4b(q, mod4(x + d)).start()
        landed[q * 4 + sx, 0] = relay0[sx, y]
        landed[q * 4 + x, 1] = relay1[sy, x]

    def tick(q):
        @pl.when(q < 4)
        def _():
            loop(0, 4, lambda i: plane(q, i))

        @pl.when(jnp.logical_and(q >= 1, q <= 4))
        def _():
            forward(q - 1)

        @pl.when(q - 2 == mine)
        def _():
            deal()

        @pl.when(q >= 3)
        def _():
            finish(q - 3)

        @pl.when(jnp.logical_and(q >= 4, q < 6))
        def _():
            advance_coarse(rows, coarse_out, coef, vel, gw, aw, (q - 4) * 8)

    loop(0, 7, tick)

    def drain(j):
        q, i = j // 4, lax.rem(j, 4)
        yj = mod4(i + q)

        @pl.when(i != x)
        def _():
            send1a(j, q, i).wait_send()
            wait4b(j)

        @pl.when(yj != y)
        def _():
            send1b(j, q, yj).wait_send()
            wait4a(j)

    loop(0, 16, drain)

    def drain_quarter(q):
        @pl.when(q != mine)
        def _():
            send2a(q, mod4(x + q)).wait_send()
            send2b(q, mod4(y - q)).wait_send()

        for d in (1, 2, 3):
            send4a(q, mod4(y + d)).wait_send()
            send4b(q, mod4(x + d)).wait_send()

    loop(0, 4, drain_quarter)
    for d in (1, 2, 3):
        send3a(mod4(x + d)).wait_send()
        send3b(mod4(y + d)).wait_send()


def fused(corner, level, vel, owner, coarse, cells, coef, gw, aw):
    spread = jnp.asarray(spread_matrix(), BF16)
    gather = jnp.asarray(spread_matrix()[:, :LANES].T.copy(), BF16)
    weights = jnp.asarray(interp_weights(), BF16)
    vmem = pl.BlockSpec(memory_space=pltpu.VMEM)
    smem = pl.BlockSpec(memory_space=pltpu.SMEM)
    dma = pltpu.SemaphoreType.DMA
    return pl.pallas_call(
        fused_kernel,
        out_shape=(
            jax.ShapeDtypeStruct((FIELDS * 64, NY), F32),
            jax.ShapeDtypeStruct((PLANES, 2, 2, UNIT, NY), BF16),
        ),
        in_specs=[smem] * 4 + [pl.BlockSpec(memory_space=pl.ANY)] + [vmem] * 7,
        out_specs=(vmem, vmem),
        scratch_shapes=[
            pltpu.VMEM((ROWS * 64, NY), F32),
            pltpu.VMEM((WIN, ROWS, WIN * NY), F32),
            pltpu.VMEM((8 * NY, 256), BF16),
            pltpu.VMEM((2, WIN, ROWS, WIDE), F32),
            pltpu.VMEM((2, EDGE, ROWS, WIDE), F32),
            pltpu.VMEM((EDGE, ROWS, 2 * LANES), F32),
            pltpu.VMEM((32, UNIT, NY), BF16),
            pltpu.VMEM((40, UNIT, NY), BF16),
            pltpu.VMEM((4, 8, NY), jnp.int32),
            pltpu.VMEM((4, 4, 8, NY), jnp.int32),
            pltpu.VMEM((2, 8, NY), jnp.int32),
            pltpu.SMEM((2, 8, NY), jnp.int32),
            pltpu.VMEM((PLANES, 2, UNIT, NY), BF16),
            pltpu.VMEM((4, 4, UNIT, NY), BF16),
            pltpu.VMEM((4, 4, UNIT, NY), BF16),
            pltpu.VMEM((17, UNIT, NY), BF16),
            pltpu.VMEM((17, UNIT, NY), BF16),
            pltpu.VMEM((4, 4, 2, UNIT, NY), BF16),
            pltpu.VMEM((4, 4, 2, UNIT, NY), BF16),
            pltpu.VMEM((4, 4, 2, UNIT, NY), BF16),
            pltpu.VMEM((4, 4, 2, UNIT, NY), BF16),
            dma,
            dma((8,)), dma((8,)),
            dma((8,)), dma((8,)),
            dma((16,)), dma((16,)), dma((16,)), dma((16,)),
            dma((4,)), dma((4,)), dma((4,)), dma((4,)),
            dma((4,)), dma((4,)), dma((4,)), dma((4,)),
            dma((16,)), dma((16,)), dma((16,)), dma((16,)),
        ],
        compiler_params=pltpu.CompilerParams(
            collective_id=0, has_side_effects=True, vmem_limit_bytes=60 * 1024 * 1024
        ),
        name="fused",
    )(corner, level, vel, owner, coarse, cells, coef, gw, aw, spread, gather, weights)


def place_kernel(landed, out):
    for j in range(PLANES):
        for h in range(2):
            first, second = unpack_pair(landed[j, h, 0])
            out[0, :, pl.ds(j * 256 + h * NY, NY)] = first[:FIELDS].astype(BF16)
            out[1, :, pl.ds(j * 256 + h * NY, NY)] = second[:FIELDS].astype(BF16)


def place(landed):
    return pl.pallas_call(
        place_kernel,
        grid=(2,),
        out_shape=jax.ShapeDtypeStruct((4, FIELDS, B**3), BF16),
        in_specs=[pl.BlockSpec((PLANES, 2, 1, UNIT, NY), lambda k: (0, 0, k, 0, 0))],
        out_specs=pl.BlockSpec((2, FIELDS, B**3), lambda k: (k, 0, 0)),
        name="place",
    )(landed)


def split(x):
    high = lax.reduce_precision(x, 8, 7)
    return high, x - high


def parameters(diffusivity, velocity, growth_weight, yield_weight):
    flow = jnp.sum(velocity)
    d = jnp.pad(diffusivity, (0, ROWS - FIELDS))
    columns = jnp.stack([1.0 - 6.0 * d - flow, d, 1.0 - 1.5 * d - 0.5 * flow, 0.25 * d])
    coef = jnp.broadcast_to(columns[:, :, None], (4, ROWS, NY))
    vel = jnp.concatenate([velocity, 0.5 * velocity])
    gh, gl = split(jnp.pad(growth_weight, ((0, 0), (0, 32 - SPEC))))
    gw = jnp.concatenate([gh, gh, gl], axis=1).astype(BF16)
    change = jnp.eye(SOOT, k=-1, dtype=F32) - jnp.eye(SOOT, dtype=F32)
    both = 0.5 * jnp.concatenate([change, yield_weight, jnp.zeros((ROWS - FIELDS, SOOT), F32)])
    ah, al = split(both)
    aw = jnp.concatenate([ah, ah, al], axis=1).astype(BF16)
    return coef, vel, gw, aw


def shards(
    coarse, fine_patches, new_owner, corners, level_tags, diffusivity, velocity, growth_weight, yield_weight
):
    coef, vel, gw, aw = parameters(diffusivity, velocity, growth_weight, yield_weight)
    flat = coarse.reshape(FIELDS * 64, NY)
    coarse_next, landed = fused(
        corners[:, 2], level_tags, vel, new_owner[:1, 0], flat, fine_patches, coef, gw, aw
    )
    return coarse_next.reshape(coarse.shape), place(landed)


def solution(mesh):
    placed = (
        P(None, "region", "patch", None),
        P(("region", "patch"), None, None),
        P(("region", "patch"), None),
        P(("region", "patch"), None),
        P(("region", "patch")),
        P(),
        P(),
        P(),
        P(),
    )
    return jax.shard_map(
        shards,
        mesh=mesh,
        in_specs=placed,
        out_specs=(P(None, "region", "patch", None), P(("region", "patch"), None, None)),
        check_vma=False,
    )
```

```python
import functools

import jax
import jax.numpy as jnp
import numpy as np
from jax import lax
from jax.experimental import pallas as pl
from jax.experimental.pallas import tpu as pltpu
from jax.sharding import PartitionSpec as P

B = 16
SOOT = 40
SPEC = 30
FIELDS = 70
ROWS = 72
WIN = 12
EDGE = 20
LANES = 384
WIDE = 512
NY = 128
PLANES = 16
PEERS = 16
UNIT = 144
MESH = pl.DeviceIdType.MESH
NEAR = (
    (0, 1), (0, 3), (1, 0), (3, 0), (0, 2), (1, 1), (1, 3), (2, 0),
    (3, 1), (3, 3), (1, 2), (2, 1), (2, 3), (3, 2), (2, 2),
)
F32 = jnp.float32
BF16 = jnp.bfloat16


def spread_matrix():
    e = np.zeros((B * B, WIDE), np.float32)
    for x in range(B):
        for y in range(B):
            e[x * B + y, (x + 2) * EDGE + y + 2] = 1.0
    return e


def interp_weights():
    m = np.zeros((EDGE, WIN), np.float32)
    for f in range(EDGE):
        parent = f // 2 + 1
        m[f, parent] = 0.75
        m[f, parent + (-1 if f % 2 == 0 else 1)] = 0.25
    v = np.zeros((256, WIDE), np.float32)
    for x in range(WIN):
        for y in range(WIN):
            v[16 * x + y, : EDGE * EDGE] = np.outer(m[:, x], m[:, y]).reshape(-1)
    return v


def dot(a, b):
    return lax.dot_general(a, b, (((1,), (0,)), ((), ())), preferred_element_type=F32)


def pack_pair(a, b):
    return jnp.concatenate([a[:64], b[:64], a[64:ROWS], b[64:ROWS]], axis=0).astype(BF16)


def unpack_pair(u):
    u = u.astype(F32)
    first = jnp.concatenate([u[:64], u[128:136]], axis=0)
    second = jnp.concatenate([u[64:128], u[136:144]], axis=0)
    return first, second


def growth(moved, gw, aw):
    soot = moved[:SOOT]
    spec = moved[SOOT:]
    sh = spec.astype(BF16)
    sl = (spec - sh.astype(F32)).astype(BF16)
    pre = dot(gw, jnp.concatenate([sh, sl, sh], axis=0))
    rate = 0.5 * jnp.tanh(0.5 * pre) + 0.5
    flux = rate * soot
    fh = flux.astype(BF16).astype(F32)
    fl = flux - fh
    return moved + dot(aw, jnp.concatenate([fh, fl, fh], axis=0).astype(BF16))


def tiled(a, n):
    return jnp.concatenate([a] * n, axis=1)


def moved_terms(c, lz, uz, lx, ux, ly, uy, own, diff, v):
    total = (lz + uz) + (lx + ux) + (ly + uy)
    return own * c + diff * total + (v[0] * lz + v[1] * lx + v[2] * ly)


def load_rows(coarse_vmem, z, x):
    return coarse_vmem[pl.ds(z * 8 + x, ROWS, stride=64), :]


def stage_coarse(coarse_hbm, coarse_vmem, sem):
    copy = pltpu.make_async_copy(coarse_hbm, coarse_vmem.at[pl.ds(0, FIELDS * 64)], sem)
    copy.start()
    coarse_vmem[FIELDS * 64 :, :] = jnp.zeros((ROWS * 64 - FIELDS * 64, NY), F32)
    return copy


def fill_rows(coarse_vmem, got, rows, edges):
    z_low, z_high, x_low, x_high = edges

    def own(z, _):
        for x in range(8):
            rows[z + 2, :, pl.ds((x + 2) * NY, NY)] = load_rows(coarse_vmem, z, x)
        a, b = unpack_pair(got[16 + z])
        rows[z + 2, :, pl.ds(0, NY)] = a * x_low
        rows[z + 2, :, pl.ds(NY, NY)] = b * x_low
        a, b = unpack_pair(got[24 + z])
        rows[z + 2, :, pl.ds(10 * NY, NY)] = a * x_high
        rows[z + 2, :, pl.ds(11 * NY, NY)] = b * x_high
        return 0

    lax.fori_loop(0, 8, own, 0)
    for x in range(WIN):
        if x < 2:
            low, high, side = 32 + x, 36 + x, x_low
        elif x < 10:
            low, high, side = x - 2, 8 + x - 2, 1.0
        else:
            low, high, side = 34 + x - 10, 38 + x - 10, x_high
        for unit, z, scale in ((low, 0, z_low * side), (high, 10, z_high * side)):
            a, b = unpack_pair(got[unit])
            rows[z, :, pl.ds(x * NY, NY)] = a * scale
            rows[z + 1, :, pl.ds(x * NY, NY)] = b * scale


def advance_coarse(rows, out, coef, vel, gw, aw, first, last):
    width = 4 * NY
    lane = lax.broadcasted_iota(jnp.int32, (ROWS, width), 1) % NY

    def step(i, _):
        z = i // 2 + 2
        base = pl.multiple_of((i % 2) * width, width)

        def part(dz, dx):
            return rows[z + dz, :, pl.ds(pl.multiple_of(base + (2 + dx) * NY, NY), width)]

        c = part(0, 0)
        pieces = [c[:, n * NY : (n + 1) * NY] for n in range(4)]
        ly = jnp.concatenate([pltpu.roll(t, 1, 1) for t in pieces], axis=1)
        uy = jnp.concatenate([pltpu.roll(t, NY - 1, 1) for t in pieces], axis=1)
        ly = jnp.where(lane == 0, 0.0, ly)
        uy = jnp.where(lane == NY - 1, 0.0, uy)
        moved = moved_terms(
            c, part(-1, 0), part(1, 0), part(0, -1), part(0, 1), ly, uy,
            tiled(coef[2], 4), tiled(coef[3], 4), (0.5 * vel[0], 0.5 * vel[1], 0.5 * vel[2]),
        )
        new = growth(moved, gw, aw)
        for n in range(4):
            at = (z - 2) * 8 + (i % 2) * 4 + n
            out[pl.ds(at, FIELDS, stride=64), :] = new[:FIELDS, n * NY : (n + 1) * NY]
        return 0

    lax.fori_loop(first, last, step, 0)


def build_windows(rows, corner, picks, window, weights):
    lane = lax.broadcasted_iota(jnp.int32, (NY, 256), 1)
    row = lax.broadcasted_iota(jnp.int32, (NY, 256), 0)
    start = jnp.where(lane < NY, corner[0, 2], corner[1, 2]) - 2
    slot = lane % NY
    for x in range(8):
        at = slot - 16 * x
        hit = jnp.logical_and(jnp.logical_and(at >= 0, at < WIN), row == start + at)
        picks[pl.ds(x * NY, NY), :] = jnp.where(hit, 1.0, 0.0).astype(BF16)
    v = weights[...]

    def group(g, _):
        z = g * 3
        lhs = rows[pl.ds(z, 3)].reshape(3 * ROWS, WIN * NY).astype(BF16)
        first = dot(lhs[:, : 8 * NY], picks[...]).astype(BF16)
        second = dot(lhs[:, 8 * NY :], picks[: 4 * NY, :]).astype(BF16)
        for n in range(2):
            cut = slice(n * NY, (n + 1) * NY)
            both = jnp.concatenate([first[:, cut], second[:, cut]], axis=1)
            window[n, pl.ds(z, 3)] = dot(both, v).reshape(3, ROWS, WIDE)
        return 0

    lax.fori_loop(0, 4, group, 0)


def build_ghosted(window, cells, ghosted, spread):
    lane = lax.broadcasted_iota(jnp.int32, (ROWS, WIDE), 1)
    x, y = lane // EDGE, lane % EDGE
    inside = (x >= 2) & (x < 18) & (y >= 2) & (y < 18)
    e = spread[...]
    pad = jnp.zeros((ROWS - FIELDS, 256), F32)

    def blend(n, f, parent, other):
        return 0.75 * window[n, parent] + 0.25 * window[n, other]

    for n in range(2):
        for f in (0, 1, 18, 19):
            parent = f // 2 + 1
            ghosted[n, f] = blend(n, f, parent, parent + (-1 if f % 2 == 0 else 1))

    def group(g, _):
        for n in range(2):
            planes = []
            for k in range(4):
                at = pl.multiple_of((g * 4 + k) * 256, 256)
                planes.append(jnp.concatenate([cells[n, :, pl.ds(at, 256)].astype(F32), pad], axis=0))
            full = dot(jnp.concatenate(planes, axis=0).astype(BF16), e)
            for k in range(4):
                f = 2 + g * 4 + k
                parent = 2 + g * 2 + k // 2
                other = parent + (-1 if k % 2 == 0 else 1)
                ghosted[n, f] = jnp.where(inside, full[k * ROWS : (k + 1) * ROWS], blend(n, f, parent, other))
        return 0

    lax.fori_loop(0, 4, group, 0)


def first_step(ghosted, z, coef, vel, gw, aw):
    moved = []
    for n in range(2):
        wide = ghosted[n, z]
        c = wide[:, :LANES]
        moved.append(
            moved_terms(
                c,
                ghosted[n, z - 1, :, :LANES],
                ghosted[n, z + 1, :, :LANES],
                pltpu.roll(c, EDGE, 1),
                pltpu.roll(wide, WIDE - EDGE, 1)[:, :LANES],
                pltpu.roll(c, 1, 1),
                pltpu.roll(c, LANES - 1, 1),
                tiled(coef[0], 3), tiled(coef[1], 3), (vel[0], vel[1], vel[2]),
            )
        )
    return growth(jnp.concatenate(moved, axis=1), gw, aw)


def second_step(once, z, coef, vel, gw, aw):
    moved = []
    for n in range(2):
        cut = pl.ds(n * LANES, LANES)
        c = once[z, :, cut]
        moved.append(
            moved_terms(
                c,
                once[z - 1, :, cut],
                once[z + 1, :, cut],
                pltpu.roll(c, EDGE, 1),
                pltpu.roll(c, LANES - EDGE, 1),
                pltpu.roll(c, 1, 1),
                pltpu.roll(c, LANES - 1, 1),
                tiled(coef[0], 3), tiled(coef[1], 3), (vel[0], vel[1], vel[2]),
            )
        )
    return growth(jnp.concatenate(moved, axis=1), gw, aw)


def remote(src, dst, send, recv, device):
    return pltpu.make_async_remote_copy(
        src_ref=src, dst_ref=dst, send_sem=send, recv_sem=recv, device_id=device, device_id_type=MESH
    )


def loop(start, stop, body):
    lax.fori_loop(start, stop, lambda i, _: (body(i), 0)[1], 0)


def prepare(diff_ref, vel, grow_ref, yield_ref, coef, grow_pad, yield_pad):
    lane = lax.broadcasted_iota(jnp.int32, (ROWS, NY), 1)
    row = lax.broadcasted_iota(jnp.int32, (ROWS, NY), 0)
    flat = jnp.concatenate([diff_ref[...], jnp.zeros((1, NY - FIELDS), F32)], axis=1)
    spread = jnp.where(lane == row, jnp.broadcast_to(flat, (ROWS, NY)), 0.0)
    d = jnp.broadcast_to(jnp.sum(spread, axis=1, keepdims=True), (ROWS, NY))
    flow = vel[0] + vel[1] + vel[2]
    coef[0] = 1.0 - 6.0 * d - flow
    coef[1] = d
    coef[2] = 1.0 - 1.5 * d - 0.5 * flow
    coef[3] = 0.25 * d
    grow_pad[...] = jnp.zeros_like(grow_pad)
    grow_pad[:SPEC, :SOOT] = grow_ref[...]
    g = jnp.transpose(grow_pad[...])[:SOOT]
    gh = g.astype(BF16).astype(F32)
    gw = jnp.concatenate([gh, gh, g - gh], axis=1).astype(BF16)
    yield_pad[...] = jnp.zeros_like(yield_pad)
    yield_pad[SOOT:FIELDS, :SOOT] = yield_ref[...]
    change = jnp.where(row == lane + 1, 1.0, 0.0) - jnp.where(row == lane, 1.0, 0.0)
    a = 0.5 * jnp.where(row < SOOT, change, yield_pad[...])[:, :SOOT]
    ah = a.astype(BF16).astype(F32)
    aw = jnp.concatenate([ah, ah, a - ah], axis=1).astype(BF16)
    return gw, aw


def offset(c):
    return (15 - c) // 4, lax.rem(15 - c, 4)


def fused_kernel(
    corner, level, vel, owner, coarse_hbm, cells, diff_ref, grow_ref, yield_ref, spread, gather, weights,
    coarse_out, landed, order_out,
    coarse_vmem, rows, picks, window, ghosted, once, coef, grow_pad, yield_pad,
    units, got, tiles, order, order_smem, packed, held, staged,
    load_sem, halo_s, halo_r, tile_s, tile_r, spread_s, spread_r, deal_s, deal_r,
):
    r, p = lax.axis_index("region"), lax.axis_index("patch")
    nr, np_ = lax.axis_size("region"), lax.axis_size("patch")
    y, x = p // 4, lax.rem(p, 4)
    up_r, down_r = lax.rem(r + 1, nr), lax.rem(r + nr - 1, nr)
    up_p, down_p = lax.rem(p + 1, np_), lax.rem(p + np_ - 1, np_)

    def peer(dy, dx):
        return lax.rem(y + dy, 4) * 4 + lax.rem(x + dx, 4)

    halo_sends = [
        ((up_r, p), 8, 8, 0),
        ((down_r, p), 0, 8, 8),
        ((r, up_p), 24, 8, 16),
        ((r, down_p), 16, 8, 24),
        ((up_r, up_p), 14, 2, 32),
        ((up_r, down_p), 8, 2, 34),
        ((down_r, up_p), 6, 2, 36),
        ((down_r, down_p), 0, 2, 38),
    ]
    barrier = pltpu.get_barrier_semaphore()
    for device, _, _, _ in halo_sends:
        pl.semaphore_signal(barrier, inc=1, device_id=device, device_id_type=MESH)

    def greet(d):
        pl.semaphore_signal(barrier, inc=1, device_id=(r, lax.rem(p + d, PEERS)), device_id_type=MESH)

    loop(1, PEERS, greet)
    load = stage_coarse(coarse_hbm, coarse_vmem, load_sem)
    tiles[p] = jnp.full((8, NY), owner[0, 0], jnp.int32)
    held[16] = jnp.zeros((UNIT, 256), BF16)
    gw, aw = prepare(diff_ref, vel, grow_ref, yield_ref, coef, grow_pad, yield_pad)
    load.wait()

    def fill(i):
        units[i] = pack_pair(load_rows(coarse_vmem, 0, i), load_rows(coarse_vmem, 1, i))
        units[8 + i] = pack_pair(load_rows(coarse_vmem, 6, i), load_rows(coarse_vmem, 7, i))
        units[16 + i] = pack_pair(load_rows(coarse_vmem, i, 0), load_rows(coarse_vmem, i, 1))
        units[24 + i] = pack_pair(load_rows(coarse_vmem, i, 6), load_rows(coarse_vmem, i, 7))

    loop(0, 8, fill)
    pl.semaphore_wait(barrier, 8 + PEERS - 1)
    halos = [
        remote(units.at[pl.ds(src, count)], got.at[pl.ds(dst, count)], halo_s.at[n], halo_r.at[n], device)
        for n, (device, src, count, dst) in enumerate(halo_sends)
    ]
    for copy in halos:
        copy.start()

    def tile(d, slot):
        return remote(tiles.at[slot], tiles.at[slot], tile_s.at[d], tile_r.at[d], (r, lax.rem(p + d, PEERS)))

    loop(1, PEERS, lambda d: tile(d, p).start())
    for copy in halos:
        copy.wait()

    edges = [jnp.where(hit, 0.0, 1.0) for hit in (r == 0, r == nr - 1, p == 0, p == np_ - 1)]
    fill_rows(coarse_vmem, got, rows, edges)
    build_windows(rows, corner, picks, window, weights)
    build_ghosted(window, cells, ghosted, spread)
    lane = lax.broadcasted_iota(jnp.int32, (ROWS, 2 * LANES), 1)
    twice = jnp.where(lane < LANES, level[0], level[1]) == 2
    for z in (1, 2, 3):
        once[z] = first_step(ghosted, z, coef, vel, gw, aw)

    def give(c):
        return remote(packed.at[c], held.at[p], spread_s.at[c], spread_r.at[c], (r, peer(*offset(c))))

    def take(c):
        dy, dx = offset(c)
        source = peer(4 - dy, 4 - dx)
        remote(packed.at[c], held.at[source], spread_s.at[c], spread_r.at[c], (r, source)).wait_recv()

    def plane(c):
        z = c + 2
        second = second_step(once, z, coef, vel, gw, aw)
        chosen = jnp.where(twice, second, once[z]).astype(BF16)
        ahead = jnp.minimum(z + 2, 18)
        once[ahead] = first_step(ghosted, ahead, coef, vel, gw, aw)
        pair = [dot(chosen[:, n * LANES : (n + 1) * LANES], gather[...]) for n in range(2)]
        packed[c] = pack_pair(*pair)

        @pl.when(c < 15)
        def _():
            give(c).start()

    loop(0, PLANES, plane)
    held[p] = packed[15]
    advance_coarse(rows, coarse_out, coef, vel, gw, aw, 0, 4)

    def settle(d):
        tile(d, p).wait_send()
        tile(d, lax.rem(p + PEERS - d, PEERS)).wait_recv()

    loop(1, PEERS, settle)
    lane = lax.broadcasted_iota(jnp.int32, (8, NY), 1)
    owners = [tiles[i] for i in range(PEERS)]
    pick = jnp.full((8, NY), 16, jnp.int32)
    for i in range(PEERS):
        slot = owners[i] * 2
        for j in range(i):
            slot = slot + jnp.where(owners[j] == owners[i], 1, 0)
        pick = jnp.where(slot == lane, i, pick)
    order[...] = pick
    order_out[...] = pick
    to_smem = pltpu.make_async_copy(order, order_smem, load_sem)
    to_smem.start()
    to_smem.wait()
    loop(0, 15, take)

    def deal(n, dy, dx):
        return remote(staged.at[n], landed.at[p], deal_s.at[n], deal_r.at[n], (r, peer(dy, dx)))

    for n, (dy, dx) in enumerate(NEAR):
        for k in range(2):
            staged[n, k] = held[order_smem[0, peer(dy, dx) * 2 + k]]
        deal(n, dy, dx).start()
    for k in range(2):
        landed[p, k] = held[order_smem[0, p * 2 + k]]
    advance_coarse(rows, coarse_out, coef, vel, gw, aw, 4, 16)
    loop(0, 15, lambda c: give(c).wait_send())
    for n, (dy, dx) in enumerate(NEAR):
        deal(n, dy, dx).wait_send()
        source = peer(4 - dy, 4 - dx)
        remote(staged.at[n], landed.at[source], deal_s.at[n], deal_r.at[n], (r, source)).wait_recv()


def fused(corner, level, vel, owner, coarse, cells, diff, grow, give):
    spread = jnp.asarray(spread_matrix(), BF16)
    gather = jnp.asarray(spread_matrix()[:, :LANES].T.copy(), BF16)
    weights = jnp.asarray(interp_weights(), BF16)
    vmem = pl.BlockSpec(memory_space=pltpu.VMEM)
    smem = pl.BlockSpec(memory_space=pltpu.SMEM)
    dma = pltpu.SemaphoreType.DMA
    return pl.pallas_call(
        fused_kernel,
        out_shape=(
            jax.ShapeDtypeStruct((FIELDS * 64, NY), F32),
            jax.ShapeDtypeStruct((PEERS, 2, UNIT, 256), BF16),
            jax.ShapeDtypeStruct((8, NY), jnp.int32),
        ),
        in_specs=[smem] * 4 + [pl.BlockSpec(memory_space=pl.ANY)] + [vmem] * 7,
        out_specs=(vmem, vmem, vmem),
        scratch_shapes=[
            pltpu.VMEM((ROWS * 64, NY), F32),
            pltpu.VMEM((WIN, ROWS, WIN * NY), F32),
            pltpu.VMEM((8 * NY, 256), BF16),
            pltpu.VMEM((2, WIN, ROWS, WIDE), F32),
            pltpu.VMEM((2, EDGE, ROWS, WIDE), F32),
            pltpu.VMEM((EDGE, ROWS, 2 * LANES), F32),
            pltpu.VMEM((4, ROWS, NY), F32),
            pltpu.VMEM((32, NY), F32),
            pltpu.VMEM((ROWS, NY), F32),
            pltpu.VMEM((32, UNIT, NY), BF16),
            pltpu.VMEM((40, UNIT, NY), BF16),
            pltpu.VMEM((PEERS, 8, NY), jnp.int32),
            pltpu.VMEM((8, NY), jnp.int32),
            pltpu.SMEM((8, NY), jnp.int32),
            pltpu.VMEM((PLANES, UNIT, 256), BF16),
            pltpu.VMEM((17, UNIT, 256), BF16),
            pltpu.VMEM((15, 2, UNIT, 256), BF16),
            dma,
            dma((8,)), dma((8,)), dma((16,)), dma((16,)), dma((16,)), dma((16,)), dma((15,)), dma((15,)),
        ],
        compiler_params=pltpu.CompilerParams(
            collective_id=0, has_side_effects=True, vmem_limit_bytes=60 * 1024 * 1024
        ),
        name="fused",
    )(corner, level, vel, owner, coarse, cells, diff, grow, give, spread, gather, weights)


def place_kernel(order, landed, out):
    p = lax.axis_index("patch")
    step = pl.program_id(0)
    for i in range(4):
        dy, dx = offset(step * 4 + i)
        four = []
        for k in range(2):
            item = jnp.minimum(order[0, p * 2 + k], PEERS - 1)
            handler = lax.rem(item // 4 + dy, 4) * 4 + lax.rem(item + dx, 4)
            four.extend(unpack_pair(landed[handler, k]))
        out[:, :, pl.ds(i * 256, 256)] = jnp.stack([f[:FIELDS] for f in four], axis=1).astype(BF16)


def place(order, landed):
    return pl.pallas_call(
        place_kernel,
        grid=(4,),
        out_shape=jax.ShapeDtypeStruct((FIELDS, 4, B**3), BF16),
        in_specs=[
            pl.BlockSpec(memory_space=pltpu.SMEM),
            pl.BlockSpec((PEERS, 2, UNIT, 256), lambda k: (0, 0, 0, 0)),
        ],
        out_specs=pl.BlockSpec((FIELDS, 4, 1024), lambda k: (0, 0, k)),
        compiler_params=pltpu.CompilerParams(vmem_limit_bytes=32 * 1024 * 1024),
        name="place",
    )(order, landed)


def shards(
    coarse, fine_patches, new_owner, corners, level_tags, diffusivity, velocity, growth_weight, yield_weight
):
    coarse_next, landed, order = fused(
        corners, level_tags, velocity, new_owner, coarse.reshape(FIELDS * 64, NY), fine_patches,
        diffusivity[None, :], growth_weight.T, yield_weight,
    )
    fine_next = jnp.transpose(place(order, landed), (1, 0, 2))
    return coarse_next.reshape(coarse.shape), fine_next


def solution(mesh):
    placed = (
        P(None, "region", "patch", None),
        P(("region", "patch"), None, None),
        P(("region", "patch"), None),
        P(("region", "patch"), None),
        P(("region", "patch")),
        P(),
        P(),
        P(),
        P(),
    )
    return jax.shard_map(
        shards,
        mesh=mesh,
        in_specs=placed,
        out_specs=(P(None, "region", "patch", None), P(("region", "patch"), None, None)),
        check_vma=False,
    )
```

```python
import functools

import jax
import jax.numpy as jnp
import numpy as np
from jax import lax
from jax.experimental import pallas as pl
from jax.experimental.pallas import tpu as pltpu
from jax.sharding import PartitionSpec as P

B = 16
SOOT = 40
SPEC = 30
FIELDS = 70
ROWS = 72
WIN = 12
EDGE = 20
LANES = 384
WIDE = 512
NY = 128
PLANES = 16
PEERS = 16
UNIT = 144
MESH = pl.DeviceIdType.MESH
F32 = jnp.float32
BF16 = jnp.bfloat16


def spread_matrix():
    e = np.zeros((B * B, WIDE), np.float32)
    for x in range(B):
        for y in range(B):
            e[x * B + y, (x + 2) * EDGE + y + 2] = 1.0
    return e


def interp_weights():
    m = np.zeros((EDGE, WIN), np.float32)
    for f in range(EDGE):
        parent = f // 2 + 1
        m[f, parent] = 0.75
        m[f, parent + (-1 if f % 2 == 0 else 1)] = 0.25
    v = np.zeros((256, WIDE), np.float32)
    for x in range(WIN):
        for y in range(WIN):
            v[16 * x + y, : EDGE * EDGE] = np.outer(m[:, x], m[:, y]).reshape(-1)
    return v


def dot(a, b):
    return lax.dot_general(a, b, (((1,), (0,)), ((), ())), preferred_element_type=F32)


def pack_pair(a, b):
    return jnp.concatenate([a[:64], b[:64], a[64:ROWS], b[64:ROWS]], axis=0).astype(BF16)


def unpack_pair(u):
    u = u.astype(F32)
    first = jnp.concatenate([u[:64], u[128:136]], axis=0)
    second = jnp.concatenate([u[64:128], u[136:144]], axis=0)
    return first, second


def growth(moved, gw, aw):
    soot = moved[:SOOT]
    spec = moved[SOOT:]
    sh = spec.astype(BF16)
    sl = (spec - sh.astype(F32)).astype(BF16)
    pre = dot(gw, jnp.concatenate([sh, sl, sh], axis=0))
    rate = 0.5 * jnp.tanh(0.5 * pre) + 0.5
    flux = rate * soot
    fh = flux.astype(BF16).astype(F32)
    fl = flux - fh
    return moved + dot(aw, jnp.concatenate([fh, fl, fh], axis=0).astype(BF16))


def tiled(a, n):
    return jnp.concatenate([a] * n, axis=1)


def moved_terms(c, lz, uz, lx, ux, ly, uy, own, diff, v):
    total = (lz + uz) + (lx + ux) + (ly + uy)
    return own * c + diff * total + (v[0] * lz + v[1] * lx + v[2] * ly)


def load_rows(coarse_vmem, z, x):
    return coarse_vmem[pl.ds(z * 8 + x, ROWS, stride=64), :]


def stage_coarse(coarse_hbm, coarse_vmem, sem):
    copy = pltpu.make_async_copy(coarse_hbm, coarse_vmem.at[pl.ds(0, FIELDS * 64)], sem)
    copy.start()
    coarse_vmem[FIELDS * 64 :, :] = jnp.zeros((ROWS * 64 - FIELDS * 64, NY), F32)
    return copy


def fill_rows(coarse_vmem, got, rows, edges):
    z_low, z_high, x_low, x_high = edges

    def own(z, _):
        for x in range(8):
            rows[z + 2, :, pl.ds((x + 2) * NY, NY)] = load_rows(coarse_vmem, z, x)
        a, b = unpack_pair(got[16 + z])
        rows[z + 2, :, pl.ds(0, NY)] = a * x_low
        rows[z + 2, :, pl.ds(NY, NY)] = b * x_low
        a, b = unpack_pair(got[24 + z])
        rows[z + 2, :, pl.ds(10 * NY, NY)] = a * x_high
        rows[z + 2, :, pl.ds(11 * NY, NY)] = b * x_high
        return 0

    lax.fori_loop(0, 8, own, 0)
    for x in range(WIN):
        if x < 2:
            low, high, side = 32 + x, 36 + x, x_low
        elif x < 10:
            low, high, side = x - 2, 8 + x - 2, 1.0
        else:
            low, high, side = 34 + x - 10, 38 + x - 10, x_high
        for unit, z, scale in ((low, 0, z_low * side), (high, 10, z_high * side)):
            a, b = unpack_pair(got[unit])
            rows[z, :, pl.ds(x * NY, NY)] = a * scale
            rows[z + 1, :, pl.ds(x * NY, NY)] = b * scale


def advance_coarse(rows, out, coef, vel, gw, aw, first, last):
    width = 4 * NY
    lane = lax.broadcasted_iota(jnp.int32, (ROWS, width), 1) % NY

    def step(i, _):
        z = i // 2 + 2
        base = pl.multiple_of((i % 2) * width, width)

        def part(dz, dx):
            return rows[z + dz, :, pl.ds(pl.multiple_of(base + (2 + dx) * NY, NY), width)]

        c = part(0, 0)
        pieces = [c[:, n * NY : (n + 1) * NY] for n in range(4)]
        ly = jnp.concatenate([pltpu.roll(t, 1, 1) for t in pieces], axis=1)
        uy = jnp.concatenate([pltpu.roll(t, NY - 1, 1) for t in pieces], axis=1)
        ly = jnp.where(lane == 0, 0.0, ly)
        uy = jnp.where(lane == NY - 1, 0.0, uy)
        moved = moved_terms(
            c, part(-1, 0), part(1, 0), part(0, -1), part(0, 1), ly, uy,
            tiled(coef[2], 4), tiled(coef[3], 4), (0.5 * vel[0], 0.5 * vel[1], 0.5 * vel[2]),
        )
        new = growth(moved, gw, aw)
        for n in range(4):
            at = (z - 2) * 8 + (i % 2) * 4 + n
            out[pl.ds(at, FIELDS, stride=64), :] = new[:FIELDS, n * NY : (n + 1) * NY]
        return 0

    lax.fori_loop(first, last, step, 0)


def build_windows(rows, corner, picks, window, weights):
    lane = lax.broadcasted_iota(jnp.int32, (NY, 256), 1)
    row = lax.broadcasted_iota(jnp.int32, (NY, 256), 0)
    start = jnp.where(lane < NY, corner[0, 2], corner[1, 2]) - 2
    slot = lane % NY
    for x in range(8):
        at = slot - 16 * x
        hit = jnp.logical_and(jnp.logical_and(at >= 0, at < WIN), row == start + at)
        picks[pl.ds(x * NY, NY), :] = jnp.where(hit, 1.0, 0.0).astype(BF16)
    v = weights[...]

    def group(g, _):
        z = g * 3
        lhs = rows[pl.ds(z, 3)].reshape(3 * ROWS, WIN * NY).astype(BF16)
        first = dot(lhs[:, : 8 * NY], picks[...]).astype(BF16)
        second = dot(lhs[:, 8 * NY :], picks[: 4 * NY, :]).astype(BF16)
        for n in range(2):
            cut = slice(n * NY, (n + 1) * NY)
            both = jnp.concatenate([first[:, cut], second[:, cut]], axis=1)
            window[n, pl.ds(z, 3)] = dot(both, v).reshape(3, ROWS, WIDE)
        return 0

    lax.fori_loop(0, 4, group, 0)


def expand(cells, ghosted, spread):
    e = spread[...]
    pad = jnp.zeros((ROWS - FIELDS, 256), F32)

    def group(g, _):
        planes = [[], []]
        for k in range(4):
            at = pl.multiple_of((g * 4 + k) * 256, 256)
            both = cells[:, :, pl.ds(at, 256)].astype(F32)
            for n in range(2):
                planes[n].append(jnp.concatenate([both[:, n, :], pad], axis=0))
        for n in range(2):
            full = dot(jnp.concatenate(planes[n], axis=0).astype(BF16), e)
            ghosted[n, pl.ds(2 + g * 4, 4)] = full.reshape(4, ROWS, WIDE)
        return 0

    lax.fori_loop(0, 4, group, 0)


def build_ghosted(window, ghosted):
    lane = lax.broadcasted_iota(jnp.int32, (ROWS, WIDE), 1)
    x, y = lane // EDGE, lane % EDGE
    inside = (x >= 2) & (x < 18) & (y >= 2) & (y < 18)

    def blend(n, f, parent, other):
        return 0.75 * window[n, parent] + 0.25 * window[n, other]

    for n in range(2):
        for f in (0, 1, 18, 19):
            parent = f // 2 + 1
            ghosted[n, f] = blend(n, f, parent, parent + (-1 if f % 2 == 0 else 1))

    def group(g, _):
        for n in range(2):
            for k in range(2):
                f = 2 + g * 2 + k
                ghosted[n, f] = jnp.where(inside, ghosted[n, f], blend(n, f, 2 + g, 1 + g + 2 * k))
        return 0

    lax.fori_loop(0, 8, group, 0)


def first_step(ghosted, z, coef, vel, gw, aw):
    moved = []
    for n in range(2):
        wide = ghosted[n, z]
        c = wide[:, :LANES]
        moved.append(
            moved_terms(
                c,
                ghosted[n, z - 1, :, :LANES],
                ghosted[n, z + 1, :, :LANES],
                pltpu.roll(c, EDGE, 1),
                pltpu.roll(wide, WIDE - EDGE, 1)[:, :LANES],
                pltpu.roll(c, 1, 1),
                pltpu.roll(c, LANES - 1, 1),
                tiled(coef[0], 3), tiled(coef[1], 3), (vel[0], vel[1], vel[2]),
            )
        )
    return growth(jnp.concatenate(moved, axis=1), gw, aw)


def second_step(once, z, coef, vel, gw, aw):
    moved = []
    for n in range(2):
        cut = pl.ds(n * LANES, LANES)
        c = once[z, :, cut]
        moved.append(
            moved_terms(
                c,
                once[z - 1, :, cut],
                once[z + 1, :, cut],
                pltpu.roll(c, EDGE, 1),
                pltpu.roll(c, LANES - EDGE, 1),
                pltpu.roll(c, 1, 1),
                pltpu.roll(c, LANES - 1, 1),
                tiled(coef[0], 3), tiled(coef[1], 3), (vel[0], vel[1], vel[2]),
            )
        )
    return growth(jnp.concatenate(moved, axis=1), gw, aw)


def remote(src, dst, send, recv, device):
    return pltpu.make_async_remote_copy(
        src_ref=src, dst_ref=dst, send_sem=send, recv_sem=recv, device_id=device, device_id_type=MESH
    )


def loop(start, stop, body):
    lax.fori_loop(start, stop, lambda i, _: (body(i), 0)[1], 0)


def prepare(diff_ref, vel, grow_ref, yield_ref, coef, grow_pad, yield_pad):
    lane = lax.broadcasted_iota(jnp.int32, (ROWS, NY), 1)
    row = lax.broadcasted_iota(jnp.int32, (ROWS, NY), 0)
    flat = jnp.concatenate([diff_ref[...], jnp.zeros((1, NY - FIELDS), F32)], axis=1)
    spread = jnp.where(lane == row, jnp.broadcast_to(flat, (ROWS, NY)), 0.0)
    d = jnp.broadcast_to(jnp.sum(spread, axis=1, keepdims=True), (ROWS, NY))
    flow = vel[0] + vel[1] + vel[2]
    coef[0] = 1.0 - 6.0 * d - flow
    coef[1] = d
    coef[2] = 1.0 - 1.5 * d - 0.5 * flow
    coef[3] = 0.25 * d
    grow_pad[...] = jnp.zeros_like(grow_pad)
    grow_pad[:SPEC, :SOOT] = grow_ref[...]
    g = jnp.transpose(grow_pad[...])[:SOOT]
    gh = g.astype(BF16).astype(F32)
    gw = jnp.concatenate([gh, gh, g - gh], axis=1).astype(BF16)
    yield_pad[...] = jnp.zeros_like(yield_pad)
    yield_pad[SOOT:FIELDS, :SOOT] = yield_ref[...]
    change = jnp.where(row == lane + 1, 1.0, 0.0) - jnp.where(row == lane, 1.0, 0.0)
    a = 0.5 * jnp.where(row < SOOT, change, yield_pad[...])[:, :SOOT]
    ah = a.astype(BF16).astype(F32)
    aw = jnp.concatenate([ah, ah, a - ah], axis=1).astype(BF16)
    return gw, aw


def offset(c):
    t = 15 - c
    return lax.rem(t // 4 + t, 4), lax.rem(t, 4)


def fused_kernel(
    corner, level, vel, owner, coarse_hbm, cells, diff_ref, grow_ref, yield_ref, spread, gather, weights,
    coarse_out, landed, order_out,
    coarse_vmem, rows, picks, window, ghosted, once, coef, grow_pad, yield_pad,
    units, got, tiles, order, order_smem, packed, held, staged, relay,
    load_sem, halo_s, halo_r, tile_s, tile_r, give_s, hold_r, stage_s, relay_s, relay_r, land_r,
):
    r, p = lax.axis_index("region"), lax.axis_index("patch")
    nr, np_ = lax.axis_size("region"), lax.axis_size("patch")
    y, x = p // 4, lax.rem(p, 4)
    up_r, down_r = lax.rem(r + 1, nr), lax.rem(r + nr - 1, nr)
    up_p, down_p = lax.rem(p + 1, np_), lax.rem(p + np_ - 1, np_)

    def peer(dy, dx):
        return lax.rem(y + dy, 4) * 4 + lax.rem(x + dx, 4)

    halo_sends = [
        ((up_r, p), 8, 8, 0),
        ((down_r, p), 0, 8, 8),
        ((r, up_p), 24, 8, 16),
        ((r, down_p), 16, 8, 24),
        ((up_r, up_p), 14, 2, 32),
        ((up_r, down_p), 8, 2, 34),
        ((down_r, up_p), 6, 2, 36),
        ((down_r, down_p), 0, 2, 38),
    ]
    barrier = pltpu.get_barrier_semaphore()
    for device, _, _, _ in halo_sends:
        pl.semaphore_signal(barrier, inc=1, device_id=device, device_id_type=MESH)

    def greet(d):
        pl.semaphore_signal(barrier, inc=1, device_id=(r, lax.rem(p + d, PEERS)), device_id_type=MESH)

    loop(1, PEERS, greet)
    load = stage_coarse(coarse_hbm, coarse_vmem, load_sem)
    tiles[p] = jnp.full((8, NY), owner[0, 0], jnp.int32)
    held[16] = jnp.zeros((2, UNIT, NY), BF16)
    gw, aw = prepare(diff_ref, vel, grow_ref, yield_ref, coef, grow_pad, yield_pad)
    load.wait()

    def fill(i):
        units[i] = pack_pair(load_rows(coarse_vmem, 0, i), load_rows(coarse_vmem, 1, i))
        units[8 + i] = pack_pair(load_rows(coarse_vmem, 6, i), load_rows(coarse_vmem, 7, i))
        units[16 + i] = pack_pair(load_rows(coarse_vmem, i, 0), load_rows(coarse_vmem, i, 1))
        units[24 + i] = pack_pair(load_rows(coarse_vmem, i, 6), load_rows(coarse_vmem, i, 7))

    loop(0, 8, fill)
    pl.semaphore_wait(barrier, 8 + PEERS - 1)
    halos = [
        remote(units.at[pl.ds(src, count)], got.at[pl.ds(dst, count)], halo_s.at[n], halo_r.at[n], device)
        for n, (device, src, count, dst) in enumerate(halo_sends)
    ]
    for copy in halos:
        copy.start()

    def tile(d, slot):
        return remote(tiles.at[slot], tiles.at[slot], tile_s.at[d], tile_r.at[d], (r, lax.rem(p + d, PEERS)))

    loop(1, PEERS, lambda d: tile(d, p).start())
    expand(cells, ghosted, spread)
    for copy in halos:
        copy.wait()

    edges = [jnp.where(hit, 0.0, 1.0) for hit in (r == 0, r == nr - 1, p == 0, p == np_ - 1)]
    fill_rows(coarse_vmem, got, rows, edges)
    build_windows(rows, corner, picks, window, weights)
    build_ghosted(window, ghosted)
    lane = lax.broadcasted_iota(jnp.int32, (ROWS, 2 * LANES), 1)
    twice = jnp.where(lane < LANES, level[0], level[1]) == 2
    for z in (1, 2, 3):
        once[z] = first_step(ghosted, z, coef, vel, gw, aw)

    def give(c):
        return remote(packed.at[c], held.at[p], give_s.at[c], hold_r.at[c], (r, peer(*offset(c))))

    def take(c):
        dy, dx = offset(c)
        source = peer(4 - dy, 4 - dx)
        remote(packed.at[c], held.at[source], give_s.at[c], hold_r.at[c], (r, source)).wait_recv()

    def plane(c):
        z = c + 2
        second = second_step(once, z, coef, vel, gw, aw)
        chosen = jnp.where(twice, second, once[z]).astype(BF16)
        ahead = jnp.minimum(z + 2, 18)
        once[ahead] = first_step(ghosted, ahead, coef, vel, gw, aw)
        pair = [dot(chosen[:, n * LANES : (n + 1) * LANES], gather[...]) for n in range(2)]
        chunk = pack_pair(*pair)
        packed[c, 0] = chunk[:, :NY]
        packed[c, 1] = chunk[:, NY:]

        @pl.when(c < 15)
        def _():
            give(c).start()

    loop(0, PLANES, plane)
    held[p] = packed[15]
    advance_coarse(rows, coarse_out, coef, vel, gw, aw, 0, 4)

    def settle(d):
        tile(d, p).wait_send()
        tile(d, lax.rem(p + PEERS - d, PEERS)).wait_recv()

    loop(1, PEERS, settle)
    lane = lax.broadcasted_iota(jnp.int32, (8, NY), 1)
    owners = [tiles[i] for i in range(PEERS)]
    pick = jnp.full((8, NY), 16, jnp.int32)
    for i in range(PEERS):
        slot = owners[i] * 2
        for j in range(i):
            slot = slot + jnp.where(owners[j] == owners[i], 1, 0)
        pick = jnp.where(slot == lane, i, pick)
    order[...] = pick
    order_out[...] = pick
    to_smem = pltpu.make_async_copy(order, order_smem, load_sem)
    to_smem.start()
    to_smem.wait()
    loop(0, 15, take)

    def send_stage(h, a, b):
        device = peer(0, a) if h == 0 else peer(a, 0)
        to, other, me = axes(h, a, b)
        return remote(staged.at[h, to, other], relay.at[h, me, other], stage_s.at[h, to, other], relay_r.at[h, me, other], (r, device))

    def axes(h, a, b):
        along, across = (x, y) if h == 0 else (y, x)
        return lax.rem(along + a, 4), lax.rem(across + b, 4), along

    def wait_stage(h, a, b):
        source, other, _ = axes(h, a, b)
        remote(
            staged.at[h, source, other], relay.at[h, source, other],
            stage_s.at[h, source, other], relay_r.at[h, source, other], (r, peer(1, 1)),
        ).wait_recv()

    def send_land(h, a, b):
        source, other, _ = axes(h, a, b)
        src = staged.at[h, source, other] if a == 0 else relay.at[h, source, other]
        handler = peer(0, a) if h == 0 else peer(a, 0)
        device = peer(b, 0) if h == 0 else peer(0, b)
        return remote(src, landed.at[handler, h], relay_s.at[h, source, other], land_r.at[h, handler], (r, device))

    def wait_land(h, a, b):
        handler = peer(b, a) if h == 0 else peer(a, b)
        remote(
            staged.at[h, 0, 0], landed.at[handler, h], relay_s.at[h, 0, 0], land_r.at[h, handler], (r, peer(1, 1))
        ).wait_recv()

    def stage(h, a, b):
        to, other, _ = axes(h, a, b)
        owner_id = peer(b, a) if h == 0 else peer(a, b)
        for k in range(2):
            staged[h, to, other, k] = held[order_smem[0, owner_id * 2 + k], h]

    for a in (1, 3, 2):
        for b in range(4):
            for h in range(2):
                stage(h, a, b)
                send_stage(h, a, b).start()
    for b in (0, 1, 3, 2):
        for h in range(2):
            stage(h, 0, b)
            if b:
                send_land(h, 0, b).start()
    for h in range(2):
        to, other, _ = axes(h, 0, 0)
        landed[p, h] = staged[h, to, other]
    begin = 4
    for a in (3, 1, 2):
        advance_coarse(rows, coarse_out, coef, vel, gw, aw, begin, begin + 4)
        begin += 4
        for b in (1, 3, 2, 0):
            for h in range(2):
                wait_stage(h, a, b)
                if b:
                    send_land(h, a, b).start()
                else:
                    source, other, _ = axes(h, a, b)
                    landed[peer(0, a) if h == 0 else peer(a, 0), h] = relay[h, source, other]

    loop(0, 15, lambda c: give(c).wait_send())
    for a in range(4):
        for b in range(4):
            for h in range(2):
                if a:
                    send_stage(h, a, b).wait_send()
                if b:
                    send_land(h, a, b).wait_send()
                    wait_land(h, a, b)


def fused(corner, level, vel, owner, coarse, cells, diff, grow, give):
    spread = jnp.asarray(spread_matrix(), BF16)
    gather = jnp.asarray(spread_matrix()[:, :LANES].T.copy(), BF16)
    weights = jnp.asarray(interp_weights(), BF16)
    vmem = pl.BlockSpec(memory_space=pltpu.VMEM)
    smem = pl.BlockSpec(memory_space=pltpu.SMEM)
    dma = pltpu.SemaphoreType.DMA
    return pl.pallas_call(
        fused_kernel,
        out_shape=(
            jax.ShapeDtypeStruct((FIELDS * 64, NY), F32),
            jax.ShapeDtypeStruct((PEERS, 2, 2, UNIT, NY), BF16),
            jax.ShapeDtypeStruct((8, NY), jnp.int32),
        ),
        in_specs=[smem] * 4 + [pl.BlockSpec(memory_space=pl.ANY)] + [vmem] * 7,
        out_specs=(vmem, vmem, vmem),
        scratch_shapes=[
            pltpu.VMEM((ROWS * 64, NY), F32),
            pltpu.VMEM((WIN, ROWS, WIN * NY), F32),
            pltpu.VMEM((8 * NY, 256), BF16),
            pltpu.VMEM((2, WIN, ROWS, WIDE), F32),
            pltpu.VMEM((2, EDGE, ROWS, WIDE), F32),
            pltpu.VMEM((EDGE, ROWS, 2 * LANES), F32),
            pltpu.VMEM((4, ROWS, NY), F32),
            pltpu.VMEM((32, NY), F32),
            pltpu.VMEM((ROWS, NY), F32),
            pltpu.VMEM((32, UNIT, NY), BF16),
            pltpu.VMEM((40, UNIT, NY), BF16),
            pltpu.VMEM((PEERS, 8, NY), jnp.int32),
            pltpu.VMEM((8, NY), jnp.int32),
            pltpu.SMEM((8, NY), jnp.int32),
            pltpu.VMEM((PLANES, 2, UNIT, NY), BF16),
            pltpu.VMEM((17, 2, UNIT, NY), BF16),
            pltpu.VMEM((2, 4, 4, 2, UNIT, NY), BF16),
            pltpu.VMEM((2, 4, 4, 2, UNIT, NY), BF16),
            dma,
            dma((8,)), dma((8,)), dma((16,)), dma((16,)),
            dma((16,)), dma((16,)),
            dma((2, 4, 4)), dma((2, 4, 4)), dma((2, 4, 4)), dma((2, 16)),
        ],
        compiler_params=pltpu.CompilerParams(
            collective_id=0, has_side_effects=True, vmem_limit_bytes=60 * 1024 * 1024
        ),
        name="fused",
    )(corner, level, vel, owner, coarse, cells, diff, grow, give, spread, gather, weights)


def place_kernel(order, landed, coarse, out, coarse_out, sem):
    p = lax.axis_index("patch")
    step = pl.program_id(0)
    copy = pltpu.make_async_copy(coarse, coarse_out, sem)

    @pl.when(step == 0)
    def _():
        copy.start()

    for i in range(4):
        dy, dx = offset(step * 4 + i)
        for h in range(2):
            four = []
            for k in range(2):
                item = jnp.minimum(order[0, p * 2 + k], PEERS - 1)
                handler = lax.rem(item // 4 + dy, 4) * 4 + lax.rem(item + dx, 4)
                four.extend(unpack_pair(landed[handler, h, k]))
            out[:, :, pl.ds(i * 256 + h * NY, NY)] = jnp.stack([f[:FIELDS] for f in four], axis=1).astype(BF16)

    @pl.when(step == 3)
    def _():
        copy.wait()


def place(order, landed, coarse):
    return pl.pallas_call(
        place_kernel,
        grid=(4,),
        out_shape=(
            jax.ShapeDtypeStruct((FIELDS, 4, B**3), BF16),
            jax.ShapeDtypeStruct((FIELDS * 64, NY), F32),
        ),
        in_specs=[
            pl.BlockSpec(memory_space=pltpu.SMEM),
            pl.BlockSpec((PEERS, 2, 2, UNIT, NY), lambda k: (0, 0, 0, 0, 0)),
            pl.BlockSpec(memory_space=pl.ANY),
        ],
        out_specs=(
            pl.BlockSpec((FIELDS, 4, 1024), lambda k: (0, 0, k)),
            pl.BlockSpec(memory_space=pl.ANY),
        ),
        scratch_shapes=[pltpu.SemaphoreType.DMA],
        compiler_params=pltpu.CompilerParams(vmem_limit_bytes=32 * 1024 * 1024),
        name="place",
    )(order, landed, coarse)


def shards(
    coarse, fine_patches, new_owner, corners, level_tags, diffusivity, velocity, growth_weight, yield_weight
):
    coarse_next, landed, order = fused(
        corners, level_tags, velocity, new_owner.T, coarse.reshape(FIELDS * 64, NY),
        jnp.transpose(fine_patches, (1, 0, 2)),
        diffusivity[None, :], growth_weight.T, yield_weight,
    )
    fine_next, coarse_next = place(order, landed, coarse_next)
    fine_next = jnp.transpose(fine_next, (1, 0, 2))
    return coarse_next.reshape(coarse.shape), fine_next


def solution(mesh):
    placed = (
        P(None, "region", "patch", None),
        P(("region", "patch"), None, None),
        P(("region", "patch"), None),
        P(("region", "patch"), None),
        P(("region", "patch")),
        P(),
        P(),
        P(),
        P(),
    )
    return jax.shard_map(
        shards,
        mesh=mesh,
        in_specs=placed,
        out_specs=(P(None, "region", "patch", None), P(("region", "patch"), None, None)),
        check_vma=False,
    )
```

```python
import functools

import jax
import jax.numpy as jnp
import numpy as np
from jax import lax
from jax.experimental import pallas as pl
from jax.experimental.pallas import tpu as pltpu
from jax.sharding import PartitionSpec as P

B = 16
SOOT = 40
SPEC = 30
FIELDS = 70
ROWS = 72
WIN = 12
EDGE = 20
LANES = 384
WIDE = 512
NY = 128
PLANES = 16
PEERS = 16
UNIT = 144
MESH = pl.DeviceIdType.MESH
F32 = jnp.float32
BF16 = jnp.bfloat16


def spread_matrix():
    e = np.zeros((B * B, WIDE), np.float32)
    for x in range(B):
        for y in range(B):
            e[x * B + y, (x + 2) * EDGE + y + 2] = 1.0
    return e


def interp_weights():
    m = np.zeros((EDGE, WIN), np.float32)
    for f in range(EDGE):
        parent = f // 2 + 1
        m[f, parent] = 0.75
        m[f, parent + (-1 if f % 2 == 0 else 1)] = 0.25
    v = np.zeros((256, WIDE), np.float32)
    for x in range(WIN):
        for y in range(WIN):
            v[16 * x + y, : EDGE * EDGE] = np.outer(m[:, x], m[:, y]).reshape(-1)
    return v


def dot(a, b):
    return lax.dot_general(a, b, (((1,), (0,)), ((), ())), preferred_element_type=F32)


def pack_pair(a, b):
    return jnp.concatenate([a[:64], b[:64], a[64:ROWS], b[64:ROWS]], axis=0).astype(BF16)


def unpack_pair(u):
    u = u.astype(F32)
    first = jnp.concatenate([u[:64], u[128:136]], axis=0)
    second = jnp.concatenate([u[64:128], u[136:144]], axis=0)
    return first, second


def growth(moved, gw, aw):
    soot = moved[:SOOT]
    spec = moved[SOOT:]
    sh = spec.astype(BF16)
    sl = (spec - sh.astype(F32)).astype(BF16)
    pre = dot(gw, jnp.concatenate([sh, sl, sh], axis=0))
    rate = 0.5 * jnp.tanh(0.5 * pre) + 0.5
    flux = rate * soot
    fh = flux.astype(BF16).astype(F32)
    fl = flux - fh
    return moved + dot(aw, jnp.concatenate([fh, fl, fh], axis=0).astype(BF16))


def tiled(a, n):
    return jnp.concatenate([a] * n, axis=1)


def moved_terms(c, lz, uz, lx, ux, ly, uy, own, diff, v):
    total = (lz + uz) + (lx + ux) + (ly + uy)
    return own * c + diff * total + (v[0] * lz + v[1] * lx + v[2] * ly)


def load_rows(coarse_vmem, z, x):
    return coarse_vmem[pl.ds(z * 8 + x, ROWS, stride=64), :]


def stage_coarse(coarse_hbm, coarse_vmem, sem):
    copy = pltpu.make_async_copy(coarse_hbm, coarse_vmem.at[pl.ds(0, FIELDS * 64)], sem)
    copy.start()
    coarse_vmem[FIELDS * 64 :, :] = jnp.zeros((ROWS * 64 - FIELDS * 64, NY), F32)
    return copy


def fill_own(coarse_vmem, rows):
    def own(z, _):
        for x in range(8):
            rows[z + 2, :, pl.ds((x + 2) * NY, NY)] = load_rows(coarse_vmem, z, x)
        return 0

    lax.fori_loop(0, 8, own, 0)


def fill_rows(got, rows, edges, part):
    z_low, z_high, x_low, x_high = edges

    def sides(z, _):
        a, b = unpack_pair(got[16 + z])
        rows[z + 2, :, pl.ds(0, NY)] = a * x_low
        rows[z + 2, :, pl.ds(NY, NY)] = b * x_low
        a, b = unpack_pair(got[24 + z])
        rows[z + 2, :, pl.ds(10 * NY, NY)] = a * x_high
        rows[z + 2, :, pl.ds(11 * NY, NY)] = b * x_high
        return 0

    lax.fori_loop(part * 4, part * 4 + 4, sides, 0)
    z, scale, face, corner = ((0, z_low, 0, 32), (10, z_high, 8, 36))[part]
    for x in range(WIN):
        unit, side = (corner + x, x_low) if x < 2 else (face + x - 2, 1.0) if x < 10 else (corner + x - 8, x_high)
        a, b = unpack_pair(got[unit])
        rows[z, :, pl.ds(x * NY, NY)] = a * (scale * side)
        rows[z + 1, :, pl.ds(x * NY, NY)] = b * (scale * side)


def advance_coarse(rows, out, coef, vel, gw, aw, first, last):
    width = 4 * NY
    lane = lax.broadcasted_iota(jnp.int32, (ROWS, width), 1) % NY

    def step(i, _):
        z = i // 2 + 2
        base = pl.multiple_of((i % 2) * width, width)

        def part(dz, dx):
            return rows[z + dz, :, pl.ds(pl.multiple_of(base + (2 + dx) * NY, NY), width)]

        c = part(0, 0)
        pieces = [c[:, n * NY : (n + 1) * NY] for n in range(4)]
        ly = jnp.concatenate([pltpu.roll(t, 1, 1) for t in pieces], axis=1)
        uy = jnp.concatenate([pltpu.roll(t, NY - 1, 1) for t in pieces], axis=1)
        ly = jnp.where(lane == 0, 0.0, ly)
        uy = jnp.where(lane == NY - 1, 0.0, uy)
        moved = moved_terms(
            c, part(-1, 0), part(1, 0), part(0, -1), part(0, 1), ly, uy,
            tiled(coef[2], 4), tiled(coef[3], 4), (0.5 * vel[0], 0.5 * vel[1], 0.5 * vel[2]),
        )
        new = growth(moved, gw, aw)
        for n in range(4):
            at = (z - 2) * 8 + (i % 2) * 4 + n
            out[pl.ds(at, FIELDS, stride=64), :] = new[:FIELDS, n * NY : (n + 1) * NY]
        return 0

    lax.fori_loop(first, last, step, 0)


def build_picks(corner, picks):
    lane = lax.broadcasted_iota(jnp.int32, (NY, 256), 1)
    row = lax.broadcasted_iota(jnp.int32, (NY, 256), 0)
    start = jnp.where(lane < NY, corner[0, 2], corner[1, 2]) - 2
    slot = lane % NY
    for x in range(8):
        at = slot - 16 * x
        hit = jnp.logical_and(jnp.logical_and(at >= 0, at < WIN), row == start + at)
        picks[pl.ds(x * NY, NY), :] = jnp.where(hit, 1.0, 0.0).astype(BF16)


def build_windows(rows, picks, window, weights, part):
    v = weights[...]
    half = pl.ds(part * 6, 6)
    low = rows[half, :, : 8 * NY].reshape(6 * ROWS, 8 * NY).astype(BF16)
    first = dot(low, picks[...]).astype(BF16)
    high = rows[half, :, 8 * NY :].reshape(6 * ROWS, 4 * NY).astype(BF16)
    second = dot(high, picks[: 4 * NY, :]).astype(BF16)
    for n in range(2):
        cut = slice(n * NY, (n + 1) * NY)
        both = jnp.concatenate([first[:, cut], second[:, cut]], axis=1)
        window[n, half] = dot(both, v).reshape(6, ROWS, WIDE)


def expand(cells, ghosted, spread):
    e = spread[...]
    pad = jnp.zeros((ROWS - FIELDS, 256), F32)

    def group(g, _):
        planes = [[], []]
        for k in range(4):
            at = pl.multiple_of((g * 4 + k) * 256, 256)
            both = cells[:, :, pl.ds(at, 256)].astype(F32)
            for n in range(2):
                planes[n].append(jnp.concatenate([both[:, n, :], pad], axis=0))
        for n in range(2):
            full = dot(jnp.concatenate(planes[n], axis=0).astype(BF16), e)
            ghosted[n, pl.ds(2 + g * 4, 4)] = full.reshape(4, ROWS, WIDE)
        return 0

    lax.fori_loop(0, 4, group, 0)


def build_ghosted(window, ghosted, part):
    lane = lax.broadcasted_iota(jnp.int32, (ROWS, WIDE), 1)
    x, y = lane // EDGE, lane % EDGE
    inside = (x >= 2) & (x < 18) & (y >= 2) & (y < 18)

    def blend(n, parent, other):
        return 0.75 * window[n, parent] + 0.25 * window[n, other]

    def frame(f, parent, other):
        for n in range(2):
            ghosted[n, f] = jnp.where(inside, ghosted[n, f], blend(n, parent, other))

    def pair(g, _):
        frame(2 + g * 2, 2 + g, 1 + g)
        frame(3 + g * 2, 2 + g, 3 + g)
        return 0

    if part == 0:
        for n in range(2):
            ghosted[n, 0] = blend(n, 1, 0)
            ghosted[n, 1] = blend(n, 1, 2)
        lax.fori_loop(0, 3, pair, 0)
        frame(8, 5, 4)
    else:
        frame(9, 5, 6)
        lax.fori_loop(4, 8, pair, 0)
        for n in range(2):
            ghosted[n, 18] = blend(n, 10, 9)
            ghosted[n, 19] = blend(n, 10, 11)


def first_step(ghosted, z, coef, vel, gw, aw):
    moved = []
    for n in range(2):
        wide = ghosted[n, z]
        c = wide[:, :LANES]
        moved.append(
            moved_terms(
                c,
                ghosted[n, z - 1, :, :LANES],
                ghosted[n, z + 1, :, :LANES],
                pltpu.roll(c, EDGE, 1),
                pltpu.roll(wide, WIDE - EDGE, 1)[:, :LANES],
                pltpu.roll(c, 1, 1),
                pltpu.roll(c, LANES - 1, 1),
                tiled(coef[0], 3), tiled(coef[1], 3), (vel[0], vel[1], vel[2]),
            )
        )
    return growth(jnp.concatenate(moved, axis=1), gw, aw)


def second_step(once, z, coef, vel, gw, aw):
    moved = []
    for n in range(2):
        cut = pl.ds(n * LANES, LANES)
        c = once[z, :, cut]
        moved.append(
            moved_terms(
                c,
                once[z - 1, :, cut],
                once[z + 1, :, cut],
                pltpu.roll(c, EDGE, 1),
                pltpu.roll(c, LANES - EDGE, 1),
                pltpu.roll(c, 1, 1),
                pltpu.roll(c, LANES - 1, 1),
                tiled(coef[0], 3), tiled(coef[1], 3), (vel[0], vel[1], vel[2]),
            )
        )
    return growth(jnp.concatenate(moved, axis=1), gw, aw)


def remote(src, dst, send, recv, device):
    return pltpu.make_async_remote_copy(
        src_ref=src, dst_ref=dst, send_sem=send, recv_sem=recv, device_id=device, device_id_type=MESH
    )


def loop(start, stop, body):
    lax.fori_loop(start, stop, lambda i, _: (body(i), 0)[1], 0)


def prepare(diff_ref, vel, grow_ref, yield_ref, coef, grow_pad, yield_pad):
    lane = lax.broadcasted_iota(jnp.int32, (ROWS, NY), 1)
    row = lax.broadcasted_iota(jnp.int32, (ROWS, NY), 0)
    flat = jnp.concatenate([diff_ref[...], jnp.zeros((1, NY - FIELDS), F32)], axis=1)
    spread = jnp.where(lane == row, jnp.broadcast_to(flat, (ROWS, NY)), 0.0)
    d = jnp.broadcast_to(jnp.sum(spread, axis=1, keepdims=True), (ROWS, NY))
    flow = vel[0] + vel[1] + vel[2]
    coef[0] = 1.0 - 6.0 * d - flow
    coef[1] = d
    coef[2] = 1.0 - 1.5 * d - 0.5 * flow
    coef[3] = 0.25 * d
    grow_pad[...] = jnp.zeros_like(grow_pad)
    grow_pad[:SPEC, :SOOT] = grow_ref[...]
    g = jnp.transpose(grow_pad[...])[:SOOT]
    gh = g.astype(BF16).astype(F32)
    gw = jnp.concatenate([gh, gh, g - gh], axis=1).astype(BF16)
    yield_pad[...] = jnp.zeros_like(yield_pad)
    yield_pad[SOOT:FIELDS, :SOOT] = yield_ref[...]
    change = jnp.where(row == lane + 1, 1.0, 0.0) - jnp.where(row == lane, 1.0, 0.0)
    a = 0.5 * jnp.where(row < SOOT, change, yield_pad[...])[:, :SOOT]
    ah = a.astype(BF16).astype(F32)
    aw = jnp.concatenate([ah, ah, a - ah], axis=1).astype(BF16)
    return gw, aw


def offset(c):
    t = 15 - c
    return lax.rem(t // 4 + t, 4), lax.rem(t, 4)


def fused_kernel(
    corner, level, vel, owner, coarse_hbm, cells, diff_ref, grow_ref, yield_ref, spread, gather, weights,
    coarse_hbm_out, landed, order_out,
    coarse_out, coarse_vmem, rows, picks, window, ghosted, once, coef, grow_pad, yield_pad,
    units, got, tiles, order, order_smem, packed, held, staged, relay,
    load_sem, halo_s, halo_r, tile_s, tile_r, give_s, hold_r, stage_s, relay_s, relay_r, land_r, local_s, out_s,
):
    r, p = lax.axis_index("region"), lax.axis_index("patch")
    nr, np_ = lax.axis_size("region"), lax.axis_size("patch")
    y, x = p // 4, lax.rem(p, 4)
    up_r, down_r = lax.rem(r + 1, nr), lax.rem(r + nr - 1, nr)
    up_p, down_p = lax.rem(p + 1, np_), lax.rem(p + np_ - 1, np_)

    def peer(dy, dx):
        return lax.rem(y + dy, 4) * 4 + lax.rem(x + dx, 4)

    halo_sends = [
        ((up_r, p), 8, 8, 0),
        ((r, up_p), 24, 4, 16),
        ((r, down_p), 16, 4, 24),
        ((up_r, up_p), 14, 2, 32),
        ((up_r, down_p), 8, 2, 34),
        ((down_r, p), 0, 8, 8),
        ((r, up_p), 28, 4, 20),
        ((r, down_p), 20, 4, 28),
        ((down_r, up_p), 6, 2, 36),
        ((down_r, down_p), 0, 2, 38),
    ]
    barrier = pltpu.get_barrier_semaphore()
    for n in (0, 1, 2, 3, 4, 5, 8, 9):
        pl.semaphore_signal(barrier, inc=1, device_id=halo_sends[n][0], device_id_type=MESH)

    def greet(d):
        pl.semaphore_signal(barrier, inc=1, device_id=(r, lax.rem(p + d, PEERS)), device_id_type=MESH)

    loop(1, PEERS, greet)
    load = stage_coarse(coarse_hbm, coarse_vmem, load_sem)
    tiles[p] = jnp.full((8, NY), owner[0, 0], jnp.int32)
    held[16] = jnp.zeros((2, UNIT, NY), BF16)
    gw, aw = prepare(diff_ref, vel, grow_ref, yield_ref, coef, grow_pad, yield_pad)
    load.wait()

    def fill(i):
        units[i] = pack_pair(load_rows(coarse_vmem, 0, i), load_rows(coarse_vmem, 1, i))
        units[8 + i] = pack_pair(load_rows(coarse_vmem, 6, i), load_rows(coarse_vmem, 7, i))
        units[16 + i] = pack_pair(load_rows(coarse_vmem, i, 0), load_rows(coarse_vmem, i, 1))
        units[24 + i] = pack_pair(load_rows(coarse_vmem, i, 6), load_rows(coarse_vmem, i, 7))

    loop(0, 8, fill)
    pl.semaphore_wait(barrier, 8 + PEERS - 1)
    halos = [
        remote(units.at[pl.ds(src, count)], got.at[pl.ds(dst, count)], halo_s.at[n], halo_r.at[n], device)
        for n, (device, src, count, dst) in enumerate(halo_sends)
    ]
    for copy in halos:
        copy.start()

    def tile(d, slot):
        return remote(tiles.at[slot], tiles.at[slot], tile_s.at[d], tile_r.at[d], (r, lax.rem(p + d, PEERS)))

    loop(1, PEERS, lambda d: tile(d, p).start())
    fill_own(coarse_vmem, rows)
    build_picks(corner, picks)
    expand(cells, ghosted, spread)
    for copy in halos[:5]:
        copy.wait()

    edges = [jnp.where(hit, 0.0, 1.0) for hit in (r == 0, r == nr - 1, p == 0, p == np_ - 1)]

    def frames(part):
        fill_rows(got, rows, edges, part)
        build_windows(rows, picks, window, weights, part)
        build_ghosted(window, ghosted, part)

    frames(0)
    lane = lax.broadcasted_iota(jnp.int32, (ROWS, 2 * LANES), 1)
    twice = jnp.where(lane < LANES, level[0], level[1]) == 2
    for z in (1, 2, 3):
        once[z] = first_step(ghosted, z, coef, vel, gw, aw)

    def give(c):
        return remote(packed.at[c], held.at[p], give_s.at[c], hold_r.at[c], (r, peer(*offset(c))))

    def take(c):
        dy, dx = offset(c)
        source = peer(4 - dy, 4 - dx)
        remote(packed.at[c], held.at[source], give_s.at[c], hold_r.at[c], (r, source)).wait_recv()

    def plane(c):
        z = c + 2
        second = second_step(once, z, coef, vel, gw, aw)
        chosen = jnp.where(twice, second, once[z]).astype(BF16)
        ahead = jnp.minimum(z + 2, 18)
        once[ahead] = first_step(ghosted, ahead, coef, vel, gw, aw)
        pair = [dot(chosen[:, n * LANES : (n + 1) * LANES], gather[...]) for n in range(2)]
        chunk = pack_pair(*pair)
        packed[c, 0] = chunk[:, :NY]
        packed[c, 1] = chunk[:, NY:]

        @pl.when(c < 15)
        def _():
            give(c).start()

    loop(0, 4, plane)
    for copy in halos[5:]:
        copy.wait()
    frames(1)
    loop(4, PLANES, plane)
    held[p] = packed[15]
    advance_coarse(rows, coarse_out, coef, vel, gw, aw, 0, 4)

    def settle(d):
        tile(d, p).wait_send()
        tile(d, lax.rem(p + PEERS - d, PEERS)).wait_recv()

    loop(1, PEERS, settle)
    lane = lax.broadcasted_iota(jnp.int32, (8, NY), 1)
    owners = [tiles[i] for i in range(PEERS)]
    pick = jnp.full((8, NY), 16, jnp.int32)
    for i in range(PEERS):
        slot = owners[i] * 2
        for j in range(i):
            slot = slot + jnp.where(owners[j] == owners[i], 1, 0)
        pick = jnp.where(slot == lane, i, pick)
    order[...] = pick
    keep_order = pltpu.make_async_copy(order, order_out, out_s.at[0])
    keep_order.start()
    to_smem = pltpu.make_async_copy(order, order_smem, load_sem)
    to_smem.start()
    to_smem.wait()
    loop(0, 15, take)

    def send_stage(h, a, b):
        device = peer(0, a) if h == 0 else peer(a, 0)
        to, other, me = axes(h, a, b)
        return remote(staged.at[h, to, other], relay.at[h, me, other], stage_s.at[h, to, other], relay_r.at[h, me, other], (r, device))

    def axes(h, a, b):
        along, across = (x, y) if h == 0 else (y, x)
        return lax.rem(along + a, 4), lax.rem(across + b, 4), along

    def wait_stage(h, a, b):
        source, other, _ = axes(h, a, b)
        remote(
            staged.at[h, source, other], relay.at[h, source, other],
            stage_s.at[h, source, other], relay_r.at[h, source, other], (r, peer(1, 1)),
        ).wait_recv()

    def send_land(h, a, b):
        source, other, _ = axes(h, a, b)
        src = staged.at[h, source, other] if a == 0 else relay.at[h, source, other]
        handler = peer(0, a) if h == 0 else peer(a, 0)
        device = peer(b, 0) if h == 0 else peer(0, b)
        return remote(src, landed.at[handler, h], relay_s.at[h, source, other], land_r.at[h, handler], (r, device))

    def wait_land(h, a, b):
        handler = peer(b, a) if h == 0 else peer(a, b)
        remote(
            staged.at[h, 0, 0], landed.at[handler, h], relay_s.at[h, 0, 0], land_r.at[h, handler], (r, peer(1, 1))
        ).wait_recv()

    def here(h, a, src, handler):
        return pltpu.make_async_copy(src, landed.at[handler, h], local_s.at[h, a])

    def stage(h, a, b):
        to, other, _ = axes(h, a, b)
        owner_id = peer(b, a) if h == 0 else peer(a, b)
        for k in range(2):
            staged[h, to, other, k] = held[order_smem[0, owner_id * 2 + k], h]

    for a in (1, 3, 2):
        for b in range(4):
            for h in range(2):
                stage(h, a, b)
                send_stage(h, a, b).start()
    for b in (0, 1, 3, 2):
        for h in range(2):
            stage(h, 0, b)
            if b:
                send_land(h, 0, b).start()
    for h in range(2):
        to, other, _ = axes(h, 0, 0)
        here(h, 0, staged.at[h, to, other], p).start()
    begin = 4
    for a in (3, 1, 2):
        advance_coarse(rows, coarse_out, coef, vel, gw, aw, begin, begin + 4)
        begin += 4
        for b in (1, 3, 2, 0):
            for h in range(2):
                wait_stage(h, a, b)
                if b:
                    send_land(h, a, b).start()
                else:
                    source, other, _ = axes(h, a, b)
                    here(h, a, relay.at[h, source, other], peer(0, a) if h == 0 else peer(a, 0)).start()

    keep_coarse = pltpu.make_async_copy(coarse_out, coarse_hbm_out, out_s.at[1])
    keep_coarse.start()
    loop(0, 15, lambda c: give(c).wait_send())
    for a in range(4):
        for b in range(4):
            for h in range(2):
                if a:
                    send_stage(h, a, b).wait_send()
                if b:
                    send_land(h, a, b).wait_send()
                    wait_land(h, a, b)
    for h in range(2):
        for a in range(4):
            here(h, a, staged.at[h, 0, 0], p).wait()
    keep_order.wait()
    keep_coarse.wait()


def fused(corner, level, vel, owner, coarse, cells, diff, grow, give):
    spread = jnp.asarray(spread_matrix(), BF16)
    gather = jnp.asarray(spread_matrix()[:, :LANES].T.copy(), BF16)
    weights = jnp.asarray(interp_weights(), BF16)
    vmem = pl.BlockSpec(memory_space=pltpu.VMEM)
    smem = pl.BlockSpec(memory_space=pltpu.SMEM)
    dma = pltpu.SemaphoreType.DMA
    return pl.pallas_call(
        fused_kernel,
        out_shape=(
            jax.ShapeDtypeStruct((FIELDS * 64, NY), F32),
            jax.ShapeDtypeStruct((PEERS, 2, 2, UNIT, NY), BF16),
            jax.ShapeDtypeStruct((8, NY), jnp.int32),
        ),
        in_specs=[smem] * 4 + [pl.BlockSpec(memory_space=pl.ANY)] + [vmem] * 7,
        out_specs=(pl.BlockSpec(memory_space=pltpu.HBM),) * 3,
        scratch_shapes=[
            pltpu.VMEM((FIELDS * 64, NY), F32),
            pltpu.VMEM((ROWS * 64, NY), F32),
            pltpu.VMEM((WIN, ROWS, WIN * NY), F32),
            pltpu.VMEM((8 * NY, 256), BF16),
            pltpu.VMEM((2, WIN, ROWS, WIDE), F32),
            pltpu.VMEM((2, EDGE, ROWS, WIDE), F32),
            pltpu.VMEM((EDGE, ROWS, 2 * LANES), F32),
            pltpu.VMEM((4, ROWS, NY), F32),
            pltpu.VMEM((32, NY), F32),
            pltpu.VMEM((ROWS, NY), F32),
            pltpu.VMEM((32, UNIT, NY), BF16),
            pltpu.VMEM((40, UNIT, NY), BF16),
            pltpu.VMEM((PEERS, 8, NY), jnp.int32),
            pltpu.VMEM((8, NY), jnp.int32),
            pltpu.SMEM((8, NY), jnp.int32),
            pltpu.VMEM((PLANES, 2, UNIT, NY), BF16),
            pltpu.VMEM((17, 2, UNIT, NY), BF16),
            pltpu.VMEM((2, 4, 4, 2, UNIT, NY), BF16),
            pltpu.VMEM((2, 4, 4, 2, UNIT, NY), BF16),
            dma,
            dma((10,)), dma((10,)), dma((16,)), dma((16,)),
            dma((16,)), dma((16,)),
            dma((2, 4, 4)), dma((2, 4, 4)), dma((2, 4, 4)), dma((2, 16)), dma((2, 4)), dma((2,)),
        ],
        compiler_params=pltpu.CompilerParams(
            collective_id=0, has_side_effects=True, vmem_limit_bytes=60 * 1024 * 1024
        ),
        name="fused",
    )(corner, level, vel, owner, coarse, cells, diff, grow, give, spread, gather, weights)


def place_kernel(order, landed, coarse, out, coarse_out, chunks, block, load_sem, sem):
    p = lax.axis_index("patch")
    step = pl.program_id(0)
    fetch = pltpu.make_async_copy(coarse, block, sem.at[0])
    keep = pltpu.make_async_copy(block, coarse_out, sem.at[1])

    def load(c, k):
        dy, dx = offset(c)
        item = jnp.minimum(order[0, p * 2 + k], PEERS - 1)
        handler = lax.rem(item // 4 + dy, 4) * 4 + lax.rem(item + dx, 4)
        return pltpu.make_async_copy(landed.at[handler, :, k], chunks.at[c, k], load_sem.at[c, k])

    @pl.when(step == 0)
    def _():
        def start(c):
            for k in range(2):
                load(c, k).start()

        loop(0, PLANES, start)
        fetch.start()

    for i in range(2):
        c = step * 2 + i
        for k in range(2):
            load(c, k).wait()
        for h in range(2):
            four = [f for k in range(2) for f in unpack_pair(chunks[c, k, h])]
            out[:, :, pl.ds(i * 256 + h * NY, NY)] = jnp.stack([f[:FIELDS] for f in four], axis=1).astype(BF16)

    @pl.when(step == 3)
    def _():
        fetch.wait()
        keep.start()

    @pl.when(step == 7)
    def _():
        keep.wait()


def place(order, landed, coarse):
    hbm = pl.BlockSpec(memory_space=pltpu.HBM)
    return pl.pallas_call(
        place_kernel,
        grid=(8,),
        out_shape=(
            jax.ShapeDtypeStruct((FIELDS, 4, B**3), BF16),
            jax.ShapeDtypeStruct((FIELDS * 64, NY), F32),
        ),
        in_specs=[pl.BlockSpec(memory_space=pltpu.SMEM), hbm, hbm],
        out_specs=(pl.BlockSpec((FIELDS, 4, 512), lambda k: (0, 0, k)), hbm),
        scratch_shapes=[
            pltpu.VMEM((PLANES, 2, 2, UNIT, NY), BF16),
            pltpu.VMEM((FIELDS * 64, NY), F32),
            pltpu.SemaphoreType.DMA((PLANES, 2)),
            pltpu.SemaphoreType.DMA((2,)),
        ],
        compiler_params=pltpu.CompilerParams(vmem_limit_bytes=60 * 1024 * 1024),
        name="place",
    )(order, landed, coarse)


def shards(
    coarse, fine_patches, new_owner, corners, level_tags, diffusivity, velocity, growth_weight, yield_weight
):
    coarse_next, landed, order = fused(
        corners, level_tags, velocity, new_owner.T, coarse.reshape(FIELDS * 64, NY),
        jnp.transpose(fine_patches, (1, 0, 2)),
        diffusivity[None, :], growth_weight.T, yield_weight,
    )
    fine_next, coarse_next = place(order, landed, coarse_next)
    fine_next = jnp.transpose(fine_next, (1, 0, 2))
    return coarse_next.reshape(coarse.shape), fine_next


def solution(mesh):
    placed = (
        P(None, "region", "patch", None),
        P(("region", "patch"), None, None),
        P(("region", "patch"), None),
        P(("region", "patch"), None),
        P(("region", "patch")),
        P(),
        P(),
        P(),
        P(),
    )
    return jax.shard_map(
        shards,
        mesh=mesh,
        in_specs=placed,
        out_specs=(P(None, "region", "patch", None), P(("region", "patch"), None, None)),
        check_vma=False,
    )
```

```python
import functools

import jax
import jax.numpy as jnp
import numpy as np
from jax import lax
from jax.experimental import pallas as pl
from jax.experimental.pallas import tpu as pltpu
from jax.sharding import PartitionSpec as P

B = 16
SOOT = 40
SPEC = 30
FIELDS = 70
ROWS = 72
WIN = 12
EDGE = 20
LANES = 384
WIDE = 512
NY = 128
PLANES = 16
PEERS = 16
COLUMN = 6
UNIT = 144
MESH = pl.DeviceIdType.MESH
F32 = jnp.float32
BF16 = jnp.bfloat16


def spread_matrix():
    e = np.zeros((B * B, WIDE), np.float32)
    for x in range(B):
        for y in range(B):
            e[x * B + y, (x + 2) * EDGE + y + 2] = 1.0
    return e


def interp_weights():
    m = np.zeros((EDGE, WIN), np.float32)
    for f in range(EDGE):
        parent = f // 2 + 1
        m[f, parent] = 0.75
        m[f, parent + (-1 if f % 2 == 0 else 1)] = 0.25
    v = np.zeros((256, WIDE), np.float32)
    for x in range(WIN):
        for y in range(WIN):
            v[16 * x + y, : EDGE * EDGE] = np.outer(m[:, x], m[:, y]).reshape(-1)
    return v


def dot(a, b):
    return lax.dot_general(a, b, (((1,), (0,)), ((), ())), preferred_element_type=F32)


def pack_pair(a, b):
    return jnp.concatenate([a[:64], b[:64], a[64:ROWS], b[64:ROWS]], axis=0).astype(BF16)


def unpack_pair(u):
    u = u.astype(F32)
    first = jnp.concatenate([u[:64], u[128:136]], axis=0)
    second = jnp.concatenate([u[64:128], u[136:144]], axis=0)
    return first, second


def growth(moved, gw, aw):
    soot = moved[:SOOT]
    spec = moved[SOOT:]
    sh = spec.astype(BF16)
    sl = (spec - sh.astype(F32)).astype(BF16)
    pre = dot(gw, jnp.concatenate([sh, sl, sh], axis=0))
    rate = 0.5 * jnp.tanh(0.5 * pre) + 0.5
    flux = rate * soot
    fh = flux.astype(BF16).astype(F32)
    fl = flux - fh
    return moved + dot(aw, jnp.concatenate([fh, fl, fh], axis=0).astype(BF16))


def tiled(a, n):
    return jnp.concatenate([a] * n, axis=1)


def moved_terms(c, lz, uz, lx, ux, ly, uy, own, diff, v):
    total = (lz + uz) + (lx + ux) + (ly + uy)
    return own * c + diff * total + (v[0] * lz + v[1] * lx + v[2] * ly)


def load_rows(coarse_vmem, z, x):
    return coarse_vmem[pl.ds(z * 8 + x, ROWS, stride=64), :]


def stage_coarse(coarse_hbm, coarse_vmem, sem):
    copy = pltpu.make_async_copy(coarse_hbm, coarse_vmem.at[pl.ds(0, FIELDS * 64)], sem)
    copy.start()
    coarse_vmem[FIELDS * 64 :, :] = jnp.zeros((ROWS * 64 - FIELDS * 64, NY), F32)
    return copy


def fill_own(coarse_vmem, rows):
    def own(z, _):
        for x in range(8):
            rows[z + 2, :, pl.ds((x + 2) * NY, NY)] = load_rows(coarse_vmem, z, x)
        return 0

    lax.fori_loop(0, 8, own, 0)


def fill_rows(got, rows, edges, part):
    z_low, z_high, x_low, x_high = edges

    def sides(z, _):
        a, b = unpack_pair(got[16 + z])
        rows[z + 2, :, pl.ds(0, NY)] = a * x_low
        rows[z + 2, :, pl.ds(NY, NY)] = b * x_low
        a, b = unpack_pair(got[24 + z])
        rows[z + 2, :, pl.ds(10 * NY, NY)] = a * x_high
        rows[z + 2, :, pl.ds(11 * NY, NY)] = b * x_high
        return 0

    lax.fori_loop(part * 4, part * 4 + 4, sides, 0)
    z, scale, face, corner = ((0, z_low, 0, 32), (10, z_high, 8, 36))[part]
    for x in range(WIN):
        unit, side = (corner + x, x_low) if x < 2 else (face + x - 2, 1.0) if x < 10 else (corner + x - 8, x_high)
        a, b = unpack_pair(got[unit])
        rows[z, :, pl.ds(x * NY, NY)] = a * (scale * side)
        rows[z + 1, :, pl.ds(x * NY, NY)] = b * (scale * side)


def advance_coarse(rows, out, coef, vel, gw, aw, first, last):
    width = 4 * NY
    lane = lax.broadcasted_iota(jnp.int32, (ROWS, width), 1) % NY

    def step(i, _):
        z = i // 2 + 2
        base = pl.multiple_of((i % 2) * width, width)

        def part(dz, dx):
            return rows[z + dz, :, pl.ds(pl.multiple_of(base + (2 + dx) * NY, NY), width)]

        c = part(0, 0)
        pieces = [c[:, n * NY : (n + 1) * NY] for n in range(4)]
        ly = jnp.concatenate([pltpu.roll(t, 1, 1) for t in pieces], axis=1)
        uy = jnp.concatenate([pltpu.roll(t, NY - 1, 1) for t in pieces], axis=1)
        ly = jnp.where(lane == 0, 0.0, ly)
        uy = jnp.where(lane == NY - 1, 0.0, uy)
        moved = moved_terms(
            c, part(-1, 0), part(1, 0), part(0, -1), part(0, 1), ly, uy,
            tiled(coef[2], 4), tiled(coef[3], 4), (0.5 * vel[0], 0.5 * vel[1], 0.5 * vel[2]),
        )
        new = growth(moved, gw, aw)
        for n in range(4):
            at = (z - 2) * 8 + (i % 2) * 4 + n
            out[pl.ds(at, FIELDS, stride=64), :] = new[:FIELDS, n * NY : (n + 1) * NY]
        return 0

    lax.fori_loop(first, last, step, 0)


def build_picks(corner, picks):
    lane = lax.broadcasted_iota(jnp.int32, (NY, 256), 1)
    row = lax.broadcasted_iota(jnp.int32, (NY, 256), 0)
    start = jnp.where(lane < NY, corner[0, 2], corner[1, 2]) - 2
    slot = lane % NY
    for x in range(8):
        at = slot - 16 * x
        hit = jnp.logical_and(jnp.logical_and(at >= 0, at < WIN), row == start + at)
        picks[pl.ds(x * NY, NY), :] = jnp.where(hit, 1.0, 0.0).astype(BF16)


def build_windows(rows, picks, window, weights, part):
    v = weights[...]
    half = pl.ds(part * 6, 6)
    low = rows[half, :, : 8 * NY].reshape(6 * ROWS, 8 * NY).astype(BF16)
    first = dot(low, picks[...]).astype(BF16)
    high = rows[half, :, 8 * NY :].reshape(6 * ROWS, 4 * NY).astype(BF16)
    second = dot(high, picks[: 4 * NY, :]).astype(BF16)
    for n in range(2):
        cut = slice(n * NY, (n + 1) * NY)
        both = jnp.concatenate([first[:, cut], second[:, cut]], axis=1)
        window[n, half] = dot(both, v).reshape(6, ROWS, WIDE)


def expand(cells, ghosted, spread):
    e = spread[...]
    pad = jnp.zeros((ROWS - FIELDS, 256), F32)

    def group(g, _):
        planes = [[], []]
        for k in range(4):
            at = pl.multiple_of((g * 4 + k) * 256, 256)
            both = cells[:, :, pl.ds(at, 256)].astype(F32)
            for n in range(2):
                planes[n].append(jnp.concatenate([both[:, n, :], pad], axis=0))
        for n in range(2):
            full = dot(jnp.concatenate(planes[n], axis=0).astype(BF16), e)
            ghosted[n, pl.ds(2 + g * 4, 4)] = full.reshape(4, ROWS, WIDE)
        return 0

    lax.fori_loop(0, 4, group, 0)


def build_ghosted(window, ghosted, part):
    lane = lax.broadcasted_iota(jnp.int32, (ROWS, WIDE), 1)
    x, y = lane // EDGE, lane % EDGE
    inside = (x >= 2) & (x < 18) & (y >= 2) & (y < 18)

    def blend(n, parent, other):
        return 0.75 * window[n, parent] + 0.25 * window[n, other]

    def frame(f, parent, other):
        for n in range(2):
            ghosted[n, f] = jnp.where(inside, ghosted[n, f], blend(n, parent, other))

    def pair(g, _):
        frame(2 + g * 2, 2 + g, 1 + g)
        frame(3 + g * 2, 2 + g, 3 + g)
        return 0

    if part == 0:
        for n in range(2):
            ghosted[n, 0] = blend(n, 1, 0)
            ghosted[n, 1] = blend(n, 1, 2)
        lax.fori_loop(0, 3, pair, 0)
        frame(8, 5, 4)
    else:
        frame(9, 5, 6)
        lax.fori_loop(4, 8, pair, 0)
        for n in range(2):
            ghosted[n, 18] = blend(n, 10, 9)
            ghosted[n, 19] = blend(n, 10, 11)


def first_step(ghosted, z, coef, vel, gw, aw):
    moved = []
    for n in range(2):
        wide = ghosted[n, z]
        c = wide[:, :LANES]
        moved.append(
            moved_terms(
                c,
                ghosted[n, z - 1, :, :LANES],
                ghosted[n, z + 1, :, :LANES],
                pltpu.roll(c, EDGE, 1),
                pltpu.roll(wide, WIDE - EDGE, 1)[:, :LANES],
                pltpu.roll(c, 1, 1),
                pltpu.roll(c, LANES - 1, 1),
                tiled(coef[0], 3), tiled(coef[1], 3), (vel[0], vel[1], vel[2]),
            )
        )
    return growth(jnp.concatenate(moved, axis=1), gw, aw)


def second_step(once, z, coef, vel, gw, aw):
    moved = []
    for n in range(2):
        cut = pl.ds(n * LANES, LANES)
        c = once[z, :, cut]
        moved.append(
            moved_terms(
                c,
                once[z - 1, :, cut],
                once[z + 1, :, cut],
                pltpu.roll(c, EDGE, 1),
                pltpu.roll(c, LANES - EDGE, 1),
                pltpu.roll(c, 1, 1),
                pltpu.roll(c, LANES - 1, 1),
                tiled(coef[0], 3), tiled(coef[1], 3), (vel[0], vel[1], vel[2]),
            )
        )
    return growth(jnp.concatenate(moved, axis=1), gw, aw)


def remote(src, dst, send, recv, device):
    return pltpu.make_async_remote_copy(
        src_ref=src, dst_ref=dst, send_sem=send, recv_sem=recv, device_id=device, device_id_type=MESH
    )


def loop(start, stop, body):
    lax.fori_loop(start, stop, lambda i, _: (body(i), 0)[1], 0)


def prepare(diff_ref, vel, grow_ref, yield_ref, coef, grow_pad, yield_pad):
    lane = lax.broadcasted_iota(jnp.int32, (ROWS, NY), 1)
    row = lax.broadcasted_iota(jnp.int32, (ROWS, NY), 0)
    flat = jnp.concatenate([diff_ref[...], jnp.zeros((1, NY - FIELDS), F32)], axis=1)
    spread = jnp.where(lane == row, jnp.broadcast_to(flat, (ROWS, NY)), 0.0)
    d = jnp.broadcast_to(jnp.sum(spread, axis=1, keepdims=True), (ROWS, NY))
    flow = vel[0] + vel[1] + vel[2]
    coef[0] = 1.0 - 6.0 * d - flow
    coef[1] = d
    coef[2] = 1.0 - 1.5 * d - 0.5 * flow
    coef[3] = 0.25 * d
    grow_pad[...] = jnp.zeros_like(grow_pad)
    grow_pad[:SPEC, :SOOT] = grow_ref[...]
    g = jnp.transpose(grow_pad[...])[:SOOT]
    gh = g.astype(BF16).astype(F32)
    gw = jnp.concatenate([gh, gh, g - gh], axis=1).astype(BF16)
    yield_pad[...] = jnp.zeros_like(yield_pad)
    yield_pad[SOOT:FIELDS, :SOOT] = yield_ref[...]
    change = jnp.where(row == lane + 1, 1.0, 0.0) - jnp.where(row == lane, 1.0, 0.0)
    a = 0.5 * jnp.where(row < SOOT, change, yield_pad[...])[:, :SOOT]
    ah = a.astype(BF16).astype(F32)
    aw = jnp.concatenate([ah, ah, a - ah], axis=1).astype(BF16)
    return gw, aw


def offset(c):
    t = 15 - c
    return lax.rem(t // 4 + t, 4), lax.rem(t, 4)


def fused_kernel(
    corner, level, vel, owner, coarse_hbm, cells, diff_ref, grow_ref, yield_ref, spread, gather, weights,
    coarse_hbm_out, landed, order_out,
    coarse_out, coarse_vmem, rows, picks, window, ghosted, once, coef, grow_pad, yield_pad,
    units, got, tiles, order, order_smem, packed, held, staged, fwd, relay01, relay02, relay03, relay11, relay12, relay13,
    load_sem, halo_s, halo_r, tile_s, tile_r, give_s, hold_r, stage_s, relay_s, relay_r, land_r, local_s, out_s,
):
    r, p = lax.axis_index("region"), lax.axis_index("patch")
    nr, np_ = lax.axis_size("region"), lax.axis_size("patch")
    y, x = p // 4, lax.rem(p, 4)
    up_r, down_r = lax.rem(r + 1, nr), lax.rem(r + nr - 1, nr)
    up_p, down_p = lax.rem(p + 1, np_), lax.rem(p + np_ - 1, np_)

    def peer(dy, dx):
        return lax.rem(y + dy, 4) * 4 + lax.rem(x + dx, 4)

    halo_sends = [
        ((up_r, p), 8, 8, 0),
        ((r, up_p), 24, 4, 16),
        ((r, down_p), 16, 4, 24),
        ((up_r, up_p), 14, 2, 32),
        ((up_r, down_p), 8, 2, 34),
        ((down_r, p), 0, 8, 8),
        ((r, up_p), 28, 4, 20),
        ((r, down_p), 20, 4, 28),
        ((down_r, up_p), 6, 2, 36),
        ((down_r, down_p), 0, 2, 38),
    ]
    barrier = pltpu.get_barrier_semaphore()
    for n in (0, 1, 2, 3, 4, 5, 8, 9):
        pl.semaphore_signal(barrier, inc=1, device_id=halo_sends[n][0], device_id_type=MESH)

    def greet(d):
        pl.semaphore_signal(barrier, inc=1, device_id=(r, lax.rem(p + d, PEERS)), device_id_type=MESH)

    loop(1, PEERS, greet)
    load = stage_coarse(coarse_hbm, coarse_vmem, load_sem)
    tiles[p] = jnp.full((8, NY), owner[0, 0], jnp.int32)
    held[16] = jnp.zeros((2, UNIT, NY), BF16)
    relay = ((None, relay01, relay02, relay03), (None, relay11, relay12, relay13))
    for h in range(2):
        for a in (1, 2, 3):
            relay[h][a][COLUMN] = jnp.zeros((UNIT, NY), BF16)
    gw, aw = prepare(diff_ref, vel, grow_ref, yield_ref, coef, grow_pad, yield_pad)
    load.wait()

    def fill(i):
        units[i] = pack_pair(load_rows(coarse_vmem, 0, i), load_rows(coarse_vmem, 1, i))
        units[8 + i] = pack_pair(load_rows(coarse_vmem, 6, i), load_rows(coarse_vmem, 7, i))
        units[16 + i] = pack_pair(load_rows(coarse_vmem, i, 0), load_rows(coarse_vmem, i, 1))
        units[24 + i] = pack_pair(load_rows(coarse_vmem, i, 6), load_rows(coarse_vmem, i, 7))

    loop(0, 8, fill)
    pl.semaphore_wait(barrier, 8 + PEERS - 1)
    halos = [
        remote(units.at[pl.ds(src, count)], got.at[pl.ds(dst, count)], halo_s.at[n], halo_r.at[n], device)
        for n, (device, src, count, dst) in enumerate(halo_sends)
    ]
    for copy in halos:
        copy.start()

    def tile(d, slot):
        return remote(tiles.at[slot], tiles.at[slot], tile_s.at[d], tile_r.at[d], (r, lax.rem(p + d, PEERS)))

    loop(1, PEERS, lambda d: tile(d, p).start())
    fill_own(coarse_vmem, rows)
    build_picks(corner, picks)
    expand(cells, ghosted, spread)
    for copy in halos[:5]:
        copy.wait()

    edges = [jnp.where(hit, 0.0, 1.0) for hit in (r == 0, r == nr - 1, p == 0, p == np_ - 1)]

    def frames(part):
        fill_rows(got, rows, edges, part)
        build_windows(rows, picks, window, weights, part)
        build_ghosted(window, ghosted, part)

    frames(0)
    lane = lax.broadcasted_iota(jnp.int32, (ROWS, 2 * LANES), 1)
    twice = jnp.where(lane < LANES, level[0], level[1]) == 2
    for z in (1, 2, 3):
        once[z] = first_step(ghosted, z, coef, vel, gw, aw)

    def give(c):
        return remote(packed.at[c], held.at[p], give_s.at[c], hold_r.at[c], (r, peer(*offset(c))))

    def take(c):
        dy, dx = offset(c)
        source = peer(4 - dy, 4 - dx)
        remote(packed.at[c], held.at[source], give_s.at[c], hold_r.at[c], (r, source)).wait_recv()

    def plane(c):
        z = c + 2
        second = second_step(once, z, coef, vel, gw, aw)
        chosen = jnp.where(twice, second, once[z]).astype(BF16)
        ahead = jnp.minimum(z + 2, 18)
        once[ahead] = first_step(ghosted, ahead, coef, vel, gw, aw)
        pair = [dot(chosen[:, n * LANES : (n + 1) * LANES], gather[...]) for n in range(2)]
        chunk = pack_pair(*pair)
        packed[c, 0] = chunk[:, :NY]
        packed[c, 1] = chunk[:, NY:]

        @pl.when(c < 15)
        def _():
            give(c).start()

    loop(0, 4, plane)
    for copy in halos[5:]:
        copy.wait()
    frames(1)
    loop(4, PLANES, plane)
    held[p] = packed[15]
    advance_coarse(rows, coarse_out, coef, vel, gw, aw, 0, 4)

    def settle(d):
        tile(d, p).wait_send()
        tile(d, lax.rem(p + PEERS - d, PEERS)).wait_recv()

    loop(1, PEERS, settle)
    lane = lax.broadcasted_iota(jnp.int32, (8, NY), 1)
    row = lax.broadcasted_iota(jnp.int32, (8, NY), 0)
    owners = [tiles[i] for i in range(PEERS)]

    def one(hit):
        return jnp.where(hit, 1, 0)

    here_y, here_x = lane // 8, lax.rem(lane // 2, 4)
    pick = jnp.full((8, NY), 16, jnp.int32)
    pick_x, pick_y = pick, pick
    ahead_x = lax.rem(lane, 2)
    ahead_y = ahead_x
    for i in range(PEERS):
        oy, ox = owners[i] // 4, lax.rem(owners[i], 4)
        rank = jnp.zeros((8, NY), jnp.int32)
        before_x, before_y = rank, rank
        for j in range(PEERS):
            jy, jx = owners[j] // 4, lax.rem(owners[j], 4)
            if j < i:
                rank = rank + one(owners[j] == owners[i])
            before_x = before_x + one((jx == ox) & (jy < oy))
            before_y = before_y + one((jy == oy) & (jx < ox))
        pick = jnp.where(owners[i] * 2 + rank == lane, i, pick)
        pick_x = jnp.where(ox * 8 + before_x + rank == lane, i, pick_x)
        pick_y = jnp.where(oy * 8 + before_y + rank == lane, i, pick_y)
        ahead_x = ahead_x + one((ox == here_x) & (oy < here_y))
        ahead_y = ahead_y + one((oy == here_y) & (ox < here_x))
    ahead_x = jnp.where(pick < 16, jnp.minimum(ahead_x, COLUMN), COLUMN)
    ahead_y = jnp.where(pick < 16, jnp.minimum(ahead_y, COLUMN), COLUMN)
    table = pick
    for n, part in enumerate((pick_x, pick_y, ahead_x, ahead_y)):
        table = jnp.where(row == n + 1, part, table)
    order[...] = table
    keep_order = pltpu.make_async_copy(order, order_out, out_s.at[0])
    keep_order.start()
    to_smem = pltpu.make_async_copy(order, order_smem, load_sem)
    to_smem.start()
    to_smem.wait()
    loop(0, 15, take)

    def along(h, a):
        return peer(0, a) if h == 0 else peer(a, 0)

    def across(h, b):
        return peer(b, 0) if h == 0 else peer(0, b)

    def send_stage(h, a):
        return remote(
            staged.at[h, a], relay[h][4 - a].at[pl.ds(0, COLUMN)], stage_s.at[h, a], relay_r.at[h, 4 - a], (r, along(h, a))
        )

    def wait_stage(h, a):
        remote(
            staged.at[h, a], relay[h][a].at[pl.ds(0, COLUMN)], stage_s.at[h, a], relay_r.at[h, a], (r, along(h, a))
        ).wait_recv()

    def send_land(h, a, b):
        handler = along(h, a)
        return remote(fwd.at[h, a, b], landed.at[handler, h], relay_s.at[h, a, b], land_r.at[h, handler], (r, across(h, b)))

    def wait_land(h, a, b):
        handler = peer(b, a) if h == 0 else peer(a, b)
        remote(fwd.at[h, a, b], landed.at[handler, h], relay_s.at[h, a, b], land_r.at[h, handler], (r, across(h, b))).wait_recv()

    def here(h, a):
        return pltpu.make_async_copy(fwd.at[h, a, 0], landed.at[along(h, a), h], local_s.at[h, a])

    for a in (1, 3, 2):
        for h in range(2):
            group = lax.rem((x if h == 0 else y) + a, 4)
            for m in range(COLUMN):
                staged[h, a, m] = held[order_smem[1 + h, group * 8 + m], h]
            send_stage(h, a).start()
    for a in (0, 3, 1, 2):
        if a:
            begin = {3: 4, 1: 8, 2: 12}[a]
            advance_coarse(rows, coarse_out, coef, vel, gw, aw, begin, begin + 4)
        for h in range(2):
            if a:
                wait_stage(h, a)
            for b in (1, 3, 2, 0):
                owner_id = across(h, b)
                for k in range(2):
                    if a:
                        fwd[h, a, b, k] = relay[h][a][jnp.clip(order_smem[3 + h, owner_id * 2 + k], 0, COLUMN)]
                    else:
                        fwd[h, a, b, k] = held[order_smem[0, owner_id * 2 + k], h]
                if b:
                    send_land(h, a, b).start()
                else:
                    here(h, a).start()
    keep_coarse = pltpu.make_async_copy(coarse_out, coarse_hbm_out, out_s.at[1])
    keep_coarse.start()
    loop(0, 15, lambda c: give(c).wait_send())
    for h in range(2):
        for a in range(4):
            if a:
                send_stage(h, a).wait_send()
            here(h, a).wait()
            for b in (1, 2, 3):
                send_land(h, a, b).wait_send()
                wait_land(h, a, b)
    keep_order.wait()
    keep_coarse.wait()


def fused(corner, level, vel, owner, coarse, cells, diff, grow, give):
    spread = jnp.asarray(spread_matrix(), BF16)
    gather = jnp.asarray(spread_matrix()[:, :LANES].T.copy(), BF16)
    weights = jnp.asarray(interp_weights(), BF16)
    vmem = pl.BlockSpec(memory_space=pltpu.VMEM)
    smem = pl.BlockSpec(memory_space=pltpu.SMEM)
    dma = pltpu.SemaphoreType.DMA
    return pl.pallas_call(
        fused_kernel,
        out_shape=(
            jax.ShapeDtypeStruct((FIELDS * 64, NY), F32),
            jax.ShapeDtypeStruct((PEERS, 2, 2, UNIT, NY), BF16),
            jax.ShapeDtypeStruct((8, NY), jnp.int32),
        ),
        in_specs=[smem] * 4 + [pl.BlockSpec(memory_space=pl.ANY)] + [vmem] * 7,
        out_specs=(pl.BlockSpec(memory_space=pltpu.HBM),) * 3,
        scratch_shapes=[
            pltpu.VMEM((FIELDS * 64, NY), F32),
            pltpu.VMEM((ROWS * 64, NY), F32),
            pltpu.VMEM((WIN, ROWS, WIN * NY), F32),
            pltpu.VMEM((8 * NY, 256), BF16),
            pltpu.VMEM((2, WIN, ROWS, WIDE), F32),
            pltpu.VMEM((2, EDGE, ROWS, WIDE), F32),
            pltpu.VMEM((EDGE, ROWS, 2 * LANES), F32),
            pltpu.VMEM((4, ROWS, NY), F32),
            pltpu.VMEM((32, NY), F32),
            pltpu.VMEM((ROWS, NY), F32),
            pltpu.VMEM((32, UNIT, NY), BF16),
            pltpu.VMEM((40, UNIT, NY), BF16),
            pltpu.VMEM((PEERS, 8, NY), jnp.int32),
            pltpu.VMEM((8, NY), jnp.int32),
            pltpu.SMEM((8, NY), jnp.int32),
            pltpu.VMEM((PLANES, 2, UNIT, NY), BF16),
            pltpu.VMEM((17, 2, UNIT, NY), BF16),
            pltpu.VMEM((2, 4, COLUMN, UNIT, NY), BF16),
            pltpu.VMEM((2, 4, 4, 2, UNIT, NY), BF16),
        ]
        + [pltpu.VMEM((COLUMN + 1, UNIT, NY), BF16)] * 6
        + [
            dma,
            dma((10,)), dma((10,)), dma((16,)), dma((16,)),
            dma((16,)), dma((16,)),
            dma((2, 4)), dma((2, 4, 4)), dma((2, 4)), dma((2, 16)), dma((2, 4)), dma((2,)),
        ],
        compiler_params=pltpu.CompilerParams(
            collective_id=0, has_side_effects=True, vmem_limit_bytes=60 * 1024 * 1024
        ),
        name="fused",
    )(corner, level, vel, owner, coarse, cells, diff, grow, give, spread, gather, weights)


def place_kernel(order, landed, coarse, out, coarse_out, chunks, block, load_sem, sem):
    p = lax.axis_index("patch")
    step = pl.program_id(0)
    fetch = pltpu.make_async_copy(coarse, block, sem.at[0])
    keep = pltpu.make_async_copy(block, coarse_out, sem.at[1])

    def load(c, k):
        dy, dx = offset(c)
        item = jnp.minimum(order[0, p * 2 + k], PEERS - 1)
        handler = lax.rem(item // 4 + dy, 4) * 4 + lax.rem(item + dx, 4)
        return pltpu.make_async_copy(landed.at[handler, :, k], chunks.at[c, k], load_sem.at[c, k])

    @pl.when(step == 0)
    def _():
        def start(c):
            for k in range(2):
                load(c, k).start()

        loop(0, PLANES, start)
        fetch.start()

    for i in range(2):
        c = step * 2 + i
        for k in range(2):
            load(c, k).wait()
        for h in range(2):
            four = [f for k in range(2) for f in unpack_pair(chunks[c, k, h])]
            out[:, :, pl.ds(i * 256 + h * NY, NY)] = jnp.stack([f[:FIELDS] for f in four], axis=1).astype(BF16)

    @pl.when(step == 3)
    def _():
        fetch.wait()
        keep.start()

    @pl.when(step == 7)
    def _():
        keep.wait()


def place(order, landed, coarse):
    hbm = pl.BlockSpec(memory_space=pltpu.HBM)
    return pl.pallas_call(
        place_kernel,
        grid=(8,),
        out_shape=(
            jax.ShapeDtypeStruct((FIELDS, 4, B**3), BF16),
            jax.ShapeDtypeStruct((FIELDS * 64, NY), F32),
        ),
        in_specs=[pl.BlockSpec(memory_space=pltpu.SMEM), hbm, hbm],
        out_specs=(pl.BlockSpec((FIELDS, 4, 512), lambda k: (0, 0, k)), hbm),
        scratch_shapes=[
            pltpu.VMEM((PLANES, 2, 2, UNIT, NY), BF16),
            pltpu.VMEM((FIELDS * 64, NY), F32),
            pltpu.SemaphoreType.DMA((PLANES, 2)),
            pltpu.SemaphoreType.DMA((2,)),
        ],
        compiler_params=pltpu.CompilerParams(vmem_limit_bytes=60 * 1024 * 1024),
        name="place",
    )(order, landed, coarse)


def shards(
    coarse, fine_patches, new_owner, corners, level_tags, diffusivity, velocity, growth_weight, yield_weight
):
    coarse_next, landed, order = fused(
        corners, level_tags, velocity, new_owner.T, coarse.reshape(FIELDS * 64, NY),
        jnp.transpose(fine_patches, (1, 0, 2)),
        diffusivity[None, :], growth_weight.T, yield_weight,
    )
    fine_next, coarse_next = place(order, landed, coarse_next)
    fine_next = jnp.transpose(fine_next, (1, 0, 2))
    return coarse_next.reshape(coarse.shape), fine_next


def solution(mesh):
    placed = (
        P(None, "region", "patch", None),
        P(("region", "patch"), None, None),
        P(("region", "patch"), None),
        P(("region", "patch"), None),
        P(("region", "patch")),
        P(),
        P(),
        P(),
        P(),
    )
    return jax.shard_map(
        shards,
        mesh=mesh,
        in_specs=placed,
        out_specs=(P(None, "region", "patch", None), P(("region", "patch"), None, None)),
        check_vma=False,
    )
```

```python
import functools

import jax
import jax.numpy as jnp
import numpy as np
from jax import lax
from jax.experimental import pallas as pl
from jax.experimental.pallas import tpu as pltpu
from jax.sharding import PartitionSpec as P

B = 16
SOOT = 40
SPEC = 30
FIELDS = 70
ROWS = 72
WIN = 12
EDGE = 20
LANES = 384
WIDE = 512
NY = 128
PLANES = 16
PEERS = 16
COLUMN = 6
UNIT = 144
MESH = pl.DeviceIdType.MESH
F32 = jnp.float32
BF16 = jnp.bfloat16


def spread_matrix():
    e = np.zeros((B * B, WIDE), np.float32)
    for x in range(B):
        for y in range(B):
            e[x * B + y, (x + 2) * EDGE + y + 2] = 1.0
    return e


def interp_weights():
    m = np.zeros((EDGE, WIN), np.float32)
    for f in range(EDGE):
        parent = f // 2 + 1
        m[f, parent] = 0.75
        m[f, parent + (-1 if f % 2 == 0 else 1)] = 0.25
    v = np.zeros((256, WIDE), np.float32)
    for x in range(WIN):
        for y in range(WIN):
            v[16 * x + y, : EDGE * EDGE] = np.outer(m[:, x], m[:, y]).reshape(-1)
    return v


def dot(a, b):
    return lax.dot_general(a, b, (((1,), (0,)), ((), ())), preferred_element_type=F32)


def pack_pair(a, b):
    return jnp.concatenate([a[:64], b[:64], a[64:ROWS], b[64:ROWS]], axis=0).astype(BF16)


def unpack_pair(u):
    u = u.astype(F32)
    first = jnp.concatenate([u[:64], u[128:136]], axis=0)
    second = jnp.concatenate([u[64:128], u[136:144]], axis=0)
    return first, second


def growth(moved, gw, aw):
    soot = moved[:SOOT]
    spec = moved[SOOT:]
    sh = spec.astype(BF16)
    sl = (spec - sh.astype(F32)).astype(BF16)
    pre = dot(gw, jnp.concatenate([sh, sl, sh], axis=0))
    rate = 0.5 * jnp.tanh(0.5 * pre) + 0.5
    flux = rate * soot
    fh = flux.astype(BF16).astype(F32)
    fl = flux - fh
    return moved + dot(aw, jnp.concatenate([fh, fl, fh], axis=0).astype(BF16))


def tiled(a, n):
    return jnp.concatenate([a] * n, axis=1)


def moved_terms(c, lz, uz, lx, ux, ly, uy, own, diff, v):
    total = (lz + uz) + (lx + ux) + (ly + uy)
    return own * c + diff * total + (v[0] * lz + v[1] * lx + v[2] * ly)


def load_rows(coarse_vmem, z, x):
    return coarse_vmem[pl.ds(z * 8 + x, ROWS, stride=64), :]


def stage_coarse(coarse_hbm, coarse_vmem, sem):
    copy = pltpu.make_async_copy(coarse_hbm, coarse_vmem.at[pl.ds(0, FIELDS * 64)], sem)
    copy.start()
    coarse_vmem[FIELDS * 64 :, :] = jnp.zeros((ROWS * 64 - FIELDS * 64, NY), F32)
    return copy


def fill_own(coarse_vmem, rows):
    def own(z, _):
        for x in range(8):
            rows[z + 2, :, pl.ds((x + 2) * NY, NY)] = load_rows(coarse_vmem, z, x)
        return 0

    lax.fori_loop(0, 8, own, 0)


def fill_rows(got, rows, edges, part):
    z_low, z_high, x_low, x_high = edges

    def sides(z, _):
        a, b = unpack_pair(got[16 + z])
        rows[z + 2, :, pl.ds(0, NY)] = a * x_low
        rows[z + 2, :, pl.ds(NY, NY)] = b * x_low
        a, b = unpack_pair(got[24 + z])
        rows[z + 2, :, pl.ds(10 * NY, NY)] = a * x_high
        rows[z + 2, :, pl.ds(11 * NY, NY)] = b * x_high
        return 0

    lax.fori_loop(part * 4, part * 4 + 4, sides, 0)
    z, scale, face, corner = ((0, z_low, 0, 32), (10, z_high, 8, 36))[part]
    for x in range(WIN):
        unit, side = (corner + x, x_low) if x < 2 else (face + x - 2, 1.0) if x < 10 else (corner + x - 8, x_high)
        a, b = unpack_pair(got[unit])
        rows[z, :, pl.ds(x * NY, NY)] = a * (scale * side)
        rows[z + 1, :, pl.ds(x * NY, NY)] = b * (scale * side)


def advance_coarse(rows, out, coef, vel, gw, aw, first, last):
    width = 4 * NY
    lane = lax.broadcasted_iota(jnp.int32, (ROWS, width), 1) % NY

    def step(i, _):
        z = i // 2 + 2
        base = pl.multiple_of((i % 2) * width, width)

        def part(dz, dx):
            return rows[z + dz, :, pl.ds(pl.multiple_of(base + (2 + dx) * NY, NY), width)]

        c = part(0, 0)
        pieces = [c[:, n * NY : (n + 1) * NY] for n in range(4)]
        ly = jnp.concatenate([pltpu.roll(t, 1, 1) for t in pieces], axis=1)
        uy = jnp.concatenate([pltpu.roll(t, NY - 1, 1) for t in pieces], axis=1)
        ly = jnp.where(lane == 0, 0.0, ly)
        uy = jnp.where(lane == NY - 1, 0.0, uy)
        moved = moved_terms(
            c, part(-1, 0), part(1, 0), part(0, -1), part(0, 1), ly, uy,
            tiled(coef[2], 4), tiled(coef[3], 4), (0.5 * vel[0], 0.5 * vel[1], 0.5 * vel[2]),
        )
        new = growth(moved, gw, aw)
        for n in range(4):
            at = (z - 2) * 8 + (i % 2) * 4 + n
            out[pl.ds(at, FIELDS, stride=64), :] = new[:FIELDS, n * NY : (n + 1) * NY]
        return 0

    lax.fori_loop(first, last, step, 0)


def build_picks(corner, picks):
    lane = lax.broadcasted_iota(jnp.int32, (NY, 256), 1)
    row = lax.broadcasted_iota(jnp.int32, (NY, 256), 0)
    start = jnp.where(lane < NY, corner[0, 2], corner[1, 2]) - 2
    slot = lane % NY
    for x in range(8):
        at = slot - 16 * x
        hit = jnp.logical_and(jnp.logical_and(at >= 0, at < WIN), row == start + at)
        picks[pl.ds(x * NY, NY), :] = jnp.where(hit, 1.0, 0.0).astype(BF16)


def build_windows(rows, picks, window, weights, part):
    v = weights[...]
    half = pl.ds(part * 6, 6)
    low = rows[half, :, : 8 * NY].reshape(6 * ROWS, 8 * NY).astype(BF16)
    first = dot(low, picks[...]).astype(BF16)
    high = rows[half, :, 8 * NY :].reshape(6 * ROWS, 4 * NY).astype(BF16)
    second = dot(high, picks[: 4 * NY, :]).astype(BF16)
    for n in range(2):
        cut = slice(n * NY, (n + 1) * NY)
        both = jnp.concatenate([first[:, cut], second[:, cut]], axis=1)
        window[n, half] = dot(both, v).reshape(6, ROWS, WIDE)


def expand(cells, ghosted, spread):
    e = spread[...]
    pad = jnp.zeros((ROWS - FIELDS, 256), F32)

    def group(g, _):
        planes = [[], []]
        for k in range(4):
            at = pl.multiple_of((g * 4 + k) * 256, 256)
            both = cells[:, :, pl.ds(at, 256)].astype(F32)
            for n in range(2):
                planes[n].append(jnp.concatenate([both[:, n, :], pad], axis=0))
        for n in range(2):
            full = dot(jnp.concatenate(planes[n], axis=0).astype(BF16), e)
            ghosted[n, pl.ds(2 + g * 4, 4)] = full.reshape(4, ROWS, WIDE)
        return 0

    lax.fori_loop(0, 4, group, 0)


def build_ghosted(window, ghosted, part):
    lane = lax.broadcasted_iota(jnp.int32, (ROWS, WIDE), 1)
    x, y = lane // EDGE, lane % EDGE
    inside = (x >= 2) & (x < 18) & (y >= 2) & (y < 18)

    def blend(n, parent, other):
        return 0.75 * window[n, parent] + 0.25 * window[n, other]

    def frame(f, parent, other):
        for n in range(2):
            ghosted[n, f] = jnp.where(inside, ghosted[n, f], blend(n, parent, other))

    def pair(g, _):
        frame(2 + g * 2, 2 + g, 1 + g)
        frame(3 + g * 2, 2 + g, 3 + g)
        return 0

    if part == 0:
        for n in range(2):
            ghosted[n, 0] = blend(n, 1, 0)
            ghosted[n, 1] = blend(n, 1, 2)
        lax.fori_loop(0, 3, pair, 0)
        frame(8, 5, 4)
    else:
        frame(9, 5, 6)
        lax.fori_loop(4, 8, pair, 0)
        for n in range(2):
            ghosted[n, 18] = blend(n, 10, 9)
            ghosted[n, 19] = blend(n, 10, 11)


def first_step(ghosted, z, coef, vel, gw, aw):
    moved = []
    for n in range(2):
        wide = ghosted[n, z]
        c = wide[:, :LANES]
        moved.append(
            moved_terms(
                c,
                ghosted[n, z - 1, :, :LANES],
                ghosted[n, z + 1, :, :LANES],
                pltpu.roll(c, EDGE, 1),
                pltpu.roll(wide, WIDE - EDGE, 1)[:, :LANES],
                pltpu.roll(c, 1, 1),
                pltpu.roll(c, LANES - 1, 1),
                tiled(coef[0], 3), tiled(coef[1], 3), (vel[0], vel[1], vel[2]),
            )
        )
    return growth(jnp.concatenate(moved, axis=1), gw, aw)


def second_step(once, z, coef, vel, gw, aw):
    moved = []
    for n in range(2):
        cut = pl.ds(n * LANES, LANES)
        c = once[z, :, cut]
        moved.append(
            moved_terms(
                c,
                once[z - 1, :, cut],
                once[z + 1, :, cut],
                pltpu.roll(c, EDGE, 1),
                pltpu.roll(c, LANES - EDGE, 1),
                pltpu.roll(c, 1, 1),
                pltpu.roll(c, LANES - 1, 1),
                tiled(coef[0], 3), tiled(coef[1], 3), (vel[0], vel[1], vel[2]),
            )
        )
    return growth(jnp.concatenate(moved, axis=1), gw, aw)


def remote(src, dst, send, recv, device):
    return pltpu.make_async_remote_copy(
        src_ref=src, dst_ref=dst, send_sem=send, recv_sem=recv, device_id=device, device_id_type=MESH
    )


def loop(start, stop, body):
    lax.fori_loop(start, stop, lambda i, _: (body(i), 0)[1], 0)


def prepare(diff_ref, vel, grow_ref, yield_ref, coef, grow_pad, yield_pad):
    lane = lax.broadcasted_iota(jnp.int32, (ROWS, NY), 1)
    row = lax.broadcasted_iota(jnp.int32, (ROWS, NY), 0)
    flat = jnp.concatenate([diff_ref[...], jnp.zeros((1, NY - FIELDS), F32)], axis=1)
    spread = jnp.where(lane == row, jnp.broadcast_to(flat, (ROWS, NY)), 0.0)
    d = jnp.broadcast_to(jnp.sum(spread, axis=1, keepdims=True), (ROWS, NY))
    flow = vel[0] + vel[1] + vel[2]
    coef[0] = 1.0 - 6.0 * d - flow
    coef[1] = d
    coef[2] = 1.0 - 1.5 * d - 0.5 * flow
    coef[3] = 0.25 * d
    grow_pad[...] = jnp.zeros_like(grow_pad)
    grow_pad[:SPEC, :SOOT] = grow_ref[...]
    g = jnp.transpose(grow_pad[...])[:SOOT]
    gh = g.astype(BF16).astype(F32)
    gw = jnp.concatenate([gh, gh, g - gh], axis=1).astype(BF16)
    yield_pad[...] = jnp.zeros_like(yield_pad)
    yield_pad[SOOT:FIELDS, :SOOT] = yield_ref[...]
    change = jnp.where(row == lane + 1, 1.0, 0.0) - jnp.where(row == lane, 1.0, 0.0)
    a = 0.5 * jnp.where(row < SOOT, change, yield_pad[...])[:, :SOOT]
    ah = a.astype(BF16).astype(F32)
    aw = jnp.concatenate([ah, ah, a - ah], axis=1).astype(BF16)
    return gw, aw


def offset(c):
    t = 15 - c
    return lax.rem(t // 4 + t, 4), lax.rem(t, 4)


def fused_kernel(
    corner, level, vel, owner, coarse_hbm, cells, diff_ref, grow_ref, yield_ref, spread, gather, weights,
    coarse_hbm_out, landed, order_out,
    coarse_out, coarse_vmem, rows, picks, window, ghosted, once, coef, grow_pad, yield_pad,
    units, got, tiles, order, order_smem, packed, held, staged, fwd, relay01, relay02, relay03, relay11, relay12, relay13,
    load_sem, halo_s, halo_r, tile_s, tile_r, give_s, hold_r, stage_s, relay_s, relay_r, land_r, local_s, out_s,
):
    r, p = lax.axis_index("region"), lax.axis_index("patch")
    nr, np_ = lax.axis_size("region"), lax.axis_size("patch")
    y, x = p // 4, lax.rem(p, 4)
    up_r, down_r = lax.rem(r + 1, nr), lax.rem(r + nr - 1, nr)
    up_p, down_p = lax.rem(p + 1, np_), lax.rem(p + np_ - 1, np_)

    def peer(dy, dx):
        return lax.rem(y + dy, 4) * 4 + lax.rem(x + dx, 4)

    halo_sends = [
        ((up_r, p), 8, 8, 0),
        ((r, up_p), 24, 4, 16),
        ((r, down_p), 16, 4, 24),
        ((up_r, up_p), 14, 2, 32),
        ((up_r, down_p), 8, 2, 34),
        ((down_r, p), 0, 8, 8),
        ((r, up_p), 28, 4, 20),
        ((r, down_p), 20, 4, 28),
        ((down_r, up_p), 6, 2, 36),
        ((down_r, down_p), 0, 2, 38),
    ]
    barrier = pltpu.get_barrier_semaphore()
    for n in (0, 1, 2, 3, 4, 5, 8, 9):
        pl.semaphore_signal(barrier, inc=1, device_id=halo_sends[n][0], device_id_type=MESH)

    def greet(d):
        pl.semaphore_signal(barrier, inc=1, device_id=(r, lax.rem(p + d, PEERS)), device_id_type=MESH)

    loop(1, PEERS, greet)
    load = stage_coarse(coarse_hbm, coarse_vmem, load_sem)
    tiles[p] = jnp.full((8, NY), owner[0, 0], jnp.int32)
    held[16] = jnp.zeros((2, UNIT, NY), BF16)
    relay = ((None, relay01, relay02, relay03), (None, relay11, relay12, relay13))
    for h in range(2):
        for a in (1, 2, 3):
            relay[h][a][COLUMN] = jnp.zeros((UNIT, NY), BF16)
    gw, aw = prepare(diff_ref, vel, grow_ref, yield_ref, coef, grow_pad, yield_pad)
    load.wait()

    def fill(i):
        units[i] = pack_pair(load_rows(coarse_vmem, 0, i), load_rows(coarse_vmem, 1, i))
        units[8 + i] = pack_pair(load_rows(coarse_vmem, 6, i), load_rows(coarse_vmem, 7, i))
        units[16 + i] = pack_pair(load_rows(coarse_vmem, i, 0), load_rows(coarse_vmem, i, 1))
        units[24 + i] = pack_pair(load_rows(coarse_vmem, i, 6), load_rows(coarse_vmem, i, 7))

    loop(0, 8, fill)
    pl.semaphore_wait(barrier, 8 + PEERS - 1)
    halos = [
        remote(units.at[pl.ds(src, count)], got.at[pl.ds(dst, count)], halo_s.at[n], halo_r.at[n], device)
        for n, (device, src, count, dst) in enumerate(halo_sends)
    ]
    for copy in halos:
        copy.start()

    def tile(d, slot):
        return remote(tiles.at[slot], tiles.at[slot], tile_s.at[d], tile_r.at[d], (r, lax.rem(p + d, PEERS)))

    loop(1, PEERS, lambda d: tile(d, p).start())
    fill_own(coarse_vmem, rows)
    build_picks(corner, picks)
    expand(cells, ghosted, spread)
    for copy in halos[:5]:
        copy.wait()

    edges = [jnp.where(hit, 0.0, 1.0) for hit in (r == 0, r == nr - 1, p == 0, p == np_ - 1)]

    def frames(part):
        fill_rows(got, rows, edges, part)
        build_windows(rows, picks, window, weights, part)
        build_ghosted(window, ghosted, part)

    frames(0)
    lane = lax.broadcasted_iota(jnp.int32, (ROWS, 2 * LANES), 1)
    twice = jnp.where(lane < LANES, level[0], level[1]) == 2
    for z in (1, 2, 3):
        once[z] = first_step(ghosted, z, coef, vel, gw, aw)

    def give(c):
        return remote(packed.at[c], held.at[p], give_s.at[c], hold_r.at[c], (r, peer(*offset(c))))

    def take(c):
        dy, dx = offset(c)
        source = peer(4 - dy, 4 - dx)
        remote(packed.at[c], held.at[source], give_s.at[c], hold_r.at[c], (r, source)).wait_recv()

    def plane(c):
        z = c + 2
        second = second_step(once, z, coef, vel, gw, aw)
        chosen = jnp.where(twice, second, once[z]).astype(BF16)
        ahead = jnp.minimum(z + 2, 18)
        once[ahead] = first_step(ghosted, ahead, coef, vel, gw, aw)
        pair = [dot(chosen[:, n * LANES : (n + 1) * LANES], gather[...]) for n in range(2)]
        chunk = pack_pair(*pair)
        packed[c, 0] = chunk[:, :NY]
        packed[c, 1] = chunk[:, NY:]

        @pl.when(c < 15)
        def _():
            give(c).start()

    loop(0, 4, plane)
    for copy in halos[5:]:
        copy.wait()
    frames(1)
    loop(4, PLANES, plane)
    held[p] = packed[15]
    advance_coarse(rows, coarse_out, coef, vel, gw, aw, 0, 4)

    def settle(d):
        tile(d, p).wait_send()
        tile(d, lax.rem(p + PEERS - d, PEERS)).wait_recv()

    loop(1, PEERS, settle)
    lane = lax.broadcasted_iota(jnp.int32, (8, NY), 1)
    row = lax.broadcasted_iota(jnp.int32, (8, NY), 0)
    owners = [tiles[i] for i in range(PEERS)]

    def one(hit):
        return jnp.where(hit, 1, 0)

    here_y, here_x = lane // 8, lax.rem(lane // 2, 4)
    pick = jnp.full((8, NY), 16, jnp.int32)
    pick_x, pick_y = pick, pick
    ahead_x = lax.rem(lane, 2)
    ahead_y = ahead_x
    for i in range(PEERS):
        oy, ox = owners[i] // 4, lax.rem(owners[i], 4)
        rank = jnp.zeros((8, NY), jnp.int32)
        before_x, before_y = rank, rank
        for j in range(PEERS):
            jy, jx = owners[j] // 4, lax.rem(owners[j], 4)
            if j < i:
                rank = rank + one(owners[j] == owners[i])
            before_x = before_x + one((jx == ox) & (jy < oy))
            before_y = before_y + one((jy == oy) & (jx < ox))
        pick = jnp.where(owners[i] * 2 + rank == lane, i, pick)
        pick_x = jnp.where(ox * 8 + before_x + rank == lane, i, pick_x)
        pick_y = jnp.where(oy * 8 + before_y + rank == lane, i, pick_y)
        ahead_x = ahead_x + one((ox == here_x) & (oy < here_y))
        ahead_y = ahead_y + one((oy == here_y) & (ox < here_x))
    ahead_x = jnp.where(pick < 16, jnp.minimum(ahead_x, COLUMN), COLUMN)
    ahead_y = jnp.where(pick < 16, jnp.minimum(ahead_y, COLUMN), COLUMN)
    table = pick
    for n, part in enumerate((pick_x, pick_y, ahead_x, ahead_y)):
        table = jnp.where(row == n + 1, part, table)
    order[...] = table
    keep_order = pltpu.make_async_copy(order, order_out, out_s.at[0])
    keep_order.start()
    to_smem = pltpu.make_async_copy(order, order_smem, load_sem)
    to_smem.start()
    to_smem.wait()
    loop(0, 15, take)

    def along(h, a):
        return peer(0, a) if h == 0 else peer(a, 0)

    def across(h, b):
        return peer(b, 0) if h == 0 else peer(0, b)

    def send_stage(h, a):
        return remote(
            staged.at[h, a], relay[h][4 - a].at[pl.ds(0, COLUMN)], stage_s.at[h, a], relay_r.at[h, 4 - a], (r, along(h, a))
        )

    def wait_stage(h, a):
        remote(
            staged.at[h, a], relay[h][a].at[pl.ds(0, COLUMN)], stage_s.at[h, a], relay_r.at[h, a], (r, along(h, a))
        ).wait_recv()

    def send_land(h, a, b):
        handler = along(h, a)
        return remote(fwd.at[h, a, b], landed.at[handler, h], relay_s.at[h, a, b], land_r.at[h, handler], (r, across(h, b)))

    def wait_land(h, a, b):
        handler = peer(b, a) if h == 0 else peer(a, b)
        remote(fwd.at[h, a, b], landed.at[handler, h], relay_s.at[h, a, b], land_r.at[h, handler], (r, across(h, b))).wait_recv()

    def here(h, a):
        return pltpu.make_async_copy(fwd.at[h, a, 0], landed.at[along(h, a), h], local_s.at[h, a])

    for a in (1, 3, 2):
        for h in range(2):
            group = lax.rem((x if h == 0 else y) + a, 4)
            for m in range(COLUMN):
                staged[h, a, m] = held[order_smem[1 + h, group * 8 + m], h]
            send_stage(h, a).start()
    for a in (0, 3, 1, 2):
        if a:
            begin = {3: 4, 1: 8, 2: 12}[a]
            advance_coarse(rows, coarse_out, coef, vel, gw, aw, begin, begin + 4)
        for h in range(2):
            if a:
                wait_stage(h, a)
            for b in (1, 3, 2, 0):
                owner_id = across(h, b)
                for k in range(2):
                    if a:
                        fwd[h, a, b, k] = relay[h][a][jnp.clip(order_smem[3 + h, owner_id * 2 + k], 0, COLUMN)]
                    else:
                        fwd[h, a, b, k] = held[order_smem[0, owner_id * 2 + k], h]
                if b:
                    send_land(h, a, b).start()
                else:
                    here(h, a).start()
    keep_coarse = pltpu.make_async_copy(coarse_out, coarse_hbm_out, out_s.at[1])
    keep_coarse.start()
    loop(0, 15, lambda c: give(c).wait_send())
    for h in range(2):
        for a in range(4):
            if a:
                send_stage(h, a).wait_send()
            here(h, a).wait()
            for b in (1, 2, 3):
                send_land(h, a, b).wait_send()
                wait_land(h, a, b)
    keep_order.wait()
    keep_coarse.wait()


def fused(corner, level, vel, owner, coarse, cells, diff, grow, give):
    spread = jnp.asarray(spread_matrix(), BF16)
    gather = jnp.asarray(spread_matrix()[:, :LANES].T.copy(), BF16)
    weights = jnp.asarray(interp_weights(), BF16)
    vmem = pl.BlockSpec(memory_space=pltpu.VMEM)
    smem = pl.BlockSpec(memory_space=pltpu.SMEM)
    dma = pltpu.SemaphoreType.DMA
    return pl.pallas_call(
        fused_kernel,
        out_shape=(
            jax.ShapeDtypeStruct((FIELDS * 64, NY), F32),
            jax.ShapeDtypeStruct((PEERS, 2, 2, UNIT, NY), BF16),
            jax.ShapeDtypeStruct((8, NY), jnp.int32),
        ),
        in_specs=[smem] * 4 + [pl.BlockSpec(memory_space=pl.ANY)] + [vmem] * 7,
        out_specs=(pl.BlockSpec(memory_space=pltpu.HBM),) * 3,
        scratch_shapes=[
            pltpu.VMEM((FIELDS * 64, NY), F32),
            pltpu.VMEM((ROWS * 64, NY), F32),
            pltpu.VMEM((WIN, ROWS, WIN * NY), F32),
            pltpu.VMEM((8 * NY, 256), BF16),
            pltpu.VMEM((2, WIN, ROWS, WIDE), F32),
            pltpu.VMEM((2, EDGE, ROWS, WIDE), F32),
            pltpu.VMEM((EDGE, ROWS, 2 * LANES), F32),
            pltpu.VMEM((4, ROWS, NY), F32),
            pltpu.VMEM((32, NY), F32),
            pltpu.VMEM((ROWS, NY), F32),
            pltpu.VMEM((32, UNIT, NY), BF16),
            pltpu.VMEM((40, UNIT, NY), BF16),
            pltpu.VMEM((PEERS, 8, NY), jnp.int32),
            pltpu.VMEM((8, NY), jnp.int32),
            pltpu.SMEM((8, NY), jnp.int32),
            pltpu.VMEM((PLANES, 2, UNIT, NY), BF16),
            pltpu.VMEM((17, 2, UNIT, NY), BF16),
            pltpu.VMEM((2, 4, COLUMN, UNIT, NY), BF16),
            pltpu.VMEM((2, 4, 4, 2, UNIT, NY), BF16),
        ]
        + [pltpu.VMEM((COLUMN + 1, UNIT, NY), BF16)] * 6
        + [
            dma,
            dma((10,)), dma((10,)), dma((16,)), dma((16,)),
            dma((16,)), dma((16,)),
            dma((2, 4)), dma((2, 4, 4)), dma((2, 4)), dma((2, 16)), dma((2, 4)), dma((2,)),
        ],
        compiler_params=pltpu.CompilerParams(
            collective_id=0, has_side_effects=True, vmem_limit_bytes=60 * 1024 * 1024
        ),
        name="fused",
    )(corner, level, vel, owner, coarse, cells, diff, grow, give, spread, gather, weights)


def place_kernel(order, landed, coarse, out, coarse_out, chunks, block, load_sem, sem):
    p = lax.axis_index("patch")
    step = pl.program_id(0)
    fetch = pltpu.make_async_copy(coarse, block, sem.at[0])
    keep = pltpu.make_async_copy(block, coarse_out, sem.at[1])

    def load(c, k):
        dy, dx = offset(c)
        item = jnp.minimum(order[0, p * 2 + k], PEERS - 1)
        handler = lax.rem(item // 4 + dy, 4) * 4 + lax.rem(item + dx, 4)
        return pltpu.make_async_copy(landed.at[handler, :, k], chunks.at[c, k], load_sem.at[c, k])

    @pl.when(step == 0)
    def _():
        def start(c):
            for k in range(2):
                load(c, k).start()

        loop(0, PLANES, start)
        fetch.start()

    for i in range(4):
        c = step * 4 + i
        for k in range(2):
            load(c, k).wait()
        for h in range(2):
            four = [f for k in range(2) for f in unpack_pair(chunks[c, k, h])]
            out[:, :, pl.ds(i * 256 + h * NY, NY)] = jnp.stack([f[:FIELDS] for f in four], axis=1).astype(BF16)

    @pl.when(step == 1)
    def _():
        fetch.wait()
        keep.start()

    @pl.when(step == 3)
    def _():
        keep.wait()


def place(order, landed, coarse):
    hbm = pl.BlockSpec(memory_space=pltpu.HBM)
    return pl.pallas_call(
        place_kernel,
        grid=(4,),
        out_shape=(
            jax.ShapeDtypeStruct((FIELDS, 4, B**3), BF16),
            jax.ShapeDtypeStruct((FIELDS * 64, NY), F32),
        ),
        in_specs=[pl.BlockSpec(memory_space=pltpu.SMEM), hbm, hbm],
        out_specs=(pl.BlockSpec((FIELDS, 4, 1024), lambda k: (0, 0, k)), hbm),
        scratch_shapes=[
            pltpu.VMEM((PLANES, 2, 2, UNIT, NY), BF16),
            pltpu.VMEM((FIELDS * 64, NY), F32),
            pltpu.SemaphoreType.DMA((PLANES, 2)),
            pltpu.SemaphoreType.DMA((2,)),
        ],
        compiler_params=pltpu.CompilerParams(vmem_limit_bytes=60 * 1024 * 1024),
        name="place",
    )(order, landed, coarse)


def shards(
    coarse, fine_patches, new_owner, corners, level_tags, diffusivity, velocity, growth_weight, yield_weight
):
    coarse_next, landed, order = fused(
        corners, level_tags, velocity, new_owner.T, coarse.reshape(FIELDS * 64, NY),
        jnp.transpose(fine_patches, (1, 0, 2)),
        diffusivity[None, :], growth_weight.T, yield_weight,
    )
    fine_next, coarse_next = place(order, landed, coarse_next)
    fine_next = jnp.transpose(fine_next, (1, 0, 2))
    return coarse_next.reshape(coarse.shape), fine_next


def solution(mesh):
    placed = (
        P(None, "region", "patch", None),
        P(("region", "patch"), None, None),
        P(("region", "patch"), None),
        P(("region", "patch"), None),
        P(("region", "patch")),
        P(),
        P(),
        P(),
        P(),
    )
    return jax.shard_map(
        shards,
        mesh=mesh,
        in_specs=placed,
        out_specs=(P(None, "region", "patch", None), P(("region", "patch"), None, None)),
        check_vma=False,
    )
```
